512 devices in a mesh: dp: 32 (over z, x), ctx: 16 (over y, core).
Axes of the slice: x: 4, y: 8, z: 8, core: 2. Of those that a mesh axis runs over, the one named last changes fastest.
Arguments:
- hidden: bfloat16 [32, 2048, 4096], P('dp', 'ctx'), may hold values from -6 to 6
- queries: bfloat16 [32, 2048, 2048], P('dp', 'ctx'), may hold values from -9 to 9
- keys: bfloat16 [32, 2048, 512], P('dp', 'ctx'), may hold values from -9 to 9
- cotangent: bfloat16 [32, 2048, 2048], P('dp', 'ctx'), may hold values from -4 to 4
- value_weight: bfloat16 [4096, 512], P('ctx'), may hold values from -0.09375 to 0.09375
- doc_ids: int32 [32, 2048], P('dp'), may hold values from 0 to 15, never falling along the last dimension, each value on 1 to 1024 neighbouring positions
- span_order: int32 [32, 32], P('dp'), may hold values from 0 to 31, each once within a row
Outputs:
- attention_out: bfloat16 [32, 2048, 2048], P('dp', 'ctx')
- query_grads: bfloat16 [32, 2048, 2048], P('dp', 'ctx')
- key_grads: bfloat16 [32, 2048, 512], P('dp', 'ctx')
- input_grads: bfloat16 [32, 2048, 4096], P('dp', 'ctx')
- weight_grads: bfloat16 [4096, 512], P('ctx')
The draws below stay inside these ranges and needn't reach their ends.
Inputs may be any that keep to these rules, and one draw needn't show every extreme that they name: `span_order`: each row lists every span of its sequence once; entries r * 2 to r * 2 + 1 are the spans of 64 positions held by ctx rank r, in order. `doc_ids`: each row never falls along the sequence; every document has at least one position and at most half of 2048, one exactly that many.
All inputs are finite; a program needn't handle non-finite values.
Results may differ from the reference program's by a relative error of at most 0.025.
The reference program's roundings to bfloat16 on the way (of `values`, `probabilities`, `dscores` and `value_grads`) count: a program that leaves them out, or rounds other values in their place, can miss the bound.
Values may be sent and summed in bfloat16 or wider, within the bound.
A program may use at most 64 MiB of HBM per device.

```python
import math
import jax
import jax.numpy as jnp
import numpy as np
from jax import lax

D = 4096
HQ = 16
KVH = 4
HD = 128
CPR = 2
TOK_DEV = 128
SEQ = 2048
NCH = 32
N_DP = 32
N_CTX = 16


def draw_queries(key, part):
    key = jax.random.fold_in(key, 7)
    first_key = jax.random.fold_in(key, 0)
    group_size = HQ // KVH
    noise = jnp.clip(jax.random.normal(first_key, (N_DP, SEQ, KVH, group_size, HD), jnp.float32), -4.0, 4.0)
    return noise.reshape(N_DP, SEQ, HQ * HD).astype(jnp.bfloat16)


def draw_keys(key, part):
    key = jax.random.fold_in(key, 13)
    first_key = jax.random.fold_in(key, 0)
    noise = jnp.clip(jax.random.normal(first_key, (N_DP, SEQ, KVH, HD), jnp.float32), -4.0, 4.0)
    return noise.reshape(N_DP, SEQ, KVH * HD).astype(jnp.bfloat16)


def block_scale(stream_key, extent, shards, smallest, top_value):
    gain, own = 1.0, jax.random.fold_in(stream_key, 6)
    for axis_at, parts in shards:
        draws = jnp.exp(jax.random.uniform(jax.random.fold_in(own, axis_at), (parts,), jnp.float32, smallest / len(shards), top_value / len(shards)))
        gain = gain * jnp.repeat(draws, extent[axis_at] // parts).reshape([-1 if axis == axis_at else 1 for axis in range(len(extent))])
    return gain


def split_up(number_of, total, most, skew):
    loads = [(1 << 20) // math.isqrt(standing ** skew) + 1 for standing in range(2, number_of + 1)]
    rest, holding = total - most - (number_of - 1), [1] * (number_of - 1)
    while rest > 0:
        movable = [i for i in range(number_of - 1) if holding[i] < most]
        pool, remaining = sum([loads[i] for i in movable]), rest
        for i in movable:
            extra = min(most - holding[i], max(1, remaining * loads[i] // pool), rest)
            holding[i] = holding[i] + extra
            rest = rest - extra
    return np.array([most] + holding)


def ragged_sizes(own_key, number_of, total, bound, skew):
    if number_of == 2:
        one = jax.random.randint(own_key, (), max(1, total - bound), min(bound, total - 1) + 1)
        return jnp.stack([one, total - one])
    sizes = jnp.asarray(split_up(number_of, total, bound, skew), jnp.int32)
    couples = (number_of - 1) // 2
    giver, taker = sizes[1:1 + 2 * couples:2], sizes[2:2 + 2 * couples:2]
    room = jnp.minimum(giver - 1, bound - taker)
    moved = jax.random.randint(jax.random.fold_in(own_key, 1), (couples,), 0, 1 << 20) % (room + 1)
    sizes = sizes.at[1:1 + 2 * couples:2].set(giver - moved).at[2:2 + 2 * couples:2].set(taker + moved)
    return sizes[jax.random.permutation(jax.random.fold_in(own_key, 2), number_of)]


def scatter_about(own_key, extent, spread, bound, pieces=(), held_as=jnp.bfloat16):
    gain = block_scale(own_key, extent, pieces, -0.22, 0.18) if pieces else 1.0
    values = jax.random.normal(own_key, extent, jnp.float32) * spread * gain
    return jnp.minimum(jnp.maximum(values, -bound), bound).astype(held_as)


def setup_inputs(seed: int = 0) -> dict:
    key_of = jax.random.split(jax.random.key(seed), 8)
    hidden = scatter_about(key_of[0], (N_DP, SEQ, D), 1.0, 6.0, ((0, 32), (1, 16)))
    queries = draw_queries(jax.random.fold_in(key_of[7], 71), 0)
    keys = draw_keys(jax.random.fold_in(key_of[7], 71), 0)
    cotangent = scatter_about(key_of[3], (N_DP, SEQ, HQ * HD), 0.25, 4.0, ((0, 32), (1, 16)))
    value_weight = scatter_about(key_of[4], (D, KVH * HD), D ** -0.5, 0.09375, ((0, 16),))
    doc_ids = jax.vmap(lambda own: jnp.searchsorted(jnp.cumsum(ragged_sizes(own, N_CTX, SEQ, SEQ // 2, 2)), jnp.arange(SEQ), side="right"))(jax.random.split(key_of[5], N_DP)).reshape((N_DP, SEQ)).astype(jnp.int32)
    span_order = jax.vmap(lambda own: jax.random.permutation(own, NCH))(jax.random.split(key_of[6], N_DP)).reshape((N_DP, NCH)).astype(jnp.int32)
    return dict(hidden=hidden, queries=queries, keys=keys, cotangent=cotangent, value_weight=value_weight, doc_ids=doc_ids, span_order=span_order)


def one_sequence(hidden, queries, keys, cotangent, value_weight, doc_list, span_list):
    span_len = TOK_DEV // CPR
    group_size = HQ // KVH
    inv_root = 1.0 / math.sqrt(HD)
    offsets = jnp.arange(span_len, dtype=jnp.int32)
    layout_docs = doc_list.reshape(-1, span_len)[span_list].reshape(SEQ)
    layout_pos = (span_list[:, None] * span_len + offsets[None, :]).reshape(SEQ)
    allowed = (layout_docs[:, None] == layout_docs[None, :]) & (layout_pos[None, :] <= layout_pos[:, None])
    values = jnp.dot(hidden, value_weight, preferred_element_type=jnp.float32).astype(jnp.bfloat16)
    query_heads = queries.reshape(SEQ, KVH, group_size, HD).transpose(1, 0, 2, 3)
    grad_heads = cotangent.reshape(SEQ, KVH, group_size, HD).transpose(1, 0, 2, 3)
    key_heads = keys.reshape(SEQ, KVH, HD).transpose(1, 0, 2)
    value_heads = values.reshape(SEQ, KVH, HD).transpose(1, 0, 2)

    def one_head(inputs):
        query_head, grad_head, key_head, value_head = inputs
        query_wide = query_head.astype(jnp.float32)
        grad_wide = grad_head.astype(jnp.float32)
        key_wide = key_head.astype(jnp.float32)
        value_wide = value_head.astype(jnp.float32)
        scores = jnp.einsum('tjd,sd->jts', query_wide, key_wide) * inv_root
        scores = jnp.where(allowed[None], scores, -jnp.inf)
        row_top = lax.optimization_barrier(jnp.max(scores, axis=2, keepdims=True))
        log_total = row_top + jnp.log(lax.optimization_barrier(jnp.sum(jnp.exp(scores - row_top), axis=2, keepdims=True)))
        probabilities = jnp.exp(scores - log_total).astype(jnp.bfloat16)
        prob_wide = probabilities.astype(jnp.float32)
        attention = jnp.einsum('jts,sd->tjd', prob_wide, value_wide).astype(jnp.bfloat16)
        delta = lax.optimization_barrier(jnp.sum(grad_wide * attention.astype(jnp.float32), axis=2))
        dprobs = jnp.einsum('tjd,sd->jts', grad_wide, value_wide)
        dscores = (prob_wide * (dprobs - delta.T[:, :, None])).astype(jnp.bfloat16)
        dscore_wide = dscores.astype(jnp.float32)
        query_grad = (jnp.einsum('jts,sd->tjd', dscore_wide, key_wide) * inv_root).astype(jnp.bfloat16)
        dscore_ranks = dscore_wide.reshape(group_size, N_CTX, TOK_DEV, SEQ)
        prob_ranks = prob_wide.reshape(group_size, N_CTX, TOK_DEV, SEQ)
        query_ranks = query_wide.reshape(N_CTX, TOK_DEV, group_size, HD)
        grad_ranks = grad_wide.reshape(N_CTX, TOK_DEV, group_size, HD)
        key_terms = (jnp.einsum('jrus,rujd->rsd', dscore_ranks, query_ranks) * inv_root).astype(jnp.bfloat16)
        value_terms = jnp.einsum('jrus,rujd->rsd', prob_ranks, grad_ranks).astype(jnp.bfloat16)
        key_grad = lax.optimization_barrier(jnp.sum(key_terms.astype(jnp.float32), axis=0)).astype(jnp.bfloat16)
        value_grad = lax.optimization_barrier(jnp.sum(value_terms.astype(jnp.float32), axis=0)).astype(jnp.bfloat16)
        return (attention, query_grad, key_grad, value_grad)
    attention, query_grad, key_grad, value_grad = lax.map(one_head, (query_heads, grad_heads, key_heads, value_heads))
    attention_out = attention.transpose(1, 0, 2, 3).reshape(SEQ, HQ * HD)
    query_grads = query_grad.transpose(1, 0, 2, 3).reshape(SEQ, HQ * HD)
    key_grads = key_grad.transpose(1, 0, 2).reshape(SEQ, KVH * HD)
    value_grads = value_grad.transpose(1, 0, 2).reshape(SEQ, KVH * HD)
    input_grads = jnp.dot(value_grads, value_weight.T, preferred_element_type=jnp.float32).astype(jnp.bfloat16)
    weight_term = jnp.dot(hidden.T, value_grads, preferred_element_type=jnp.float32)
    return (attention_out, query_grads, key_grads, input_grads, weight_term)

def reference(hidden, queries, keys, cotangent, value_weight, doc_ids, span_order):

    def run_one(carry, inputs):
        hidden_one, query_one, key_one, grad_one, doc_one, span_one = inputs
        attention_out, query_grads, key_grads, input_grads, weight_term = one_sequence(hidden_one, query_one, key_one, grad_one, value_weight, doc_one, span_one)
        return (carry + weight_term, (attention_out, query_grads, key_grads, input_grads))
    start = jnp.zeros((D, KVH * HD), jnp.float32)
    weight_total, stacked = lax.scan(run_one, start, (hidden, queries, keys, cotangent, doc_ids, span_order))
    attention_out, query_grads, key_grads, input_grads = stacked
    weight_grads = (weight_total / N_DP).astype(jnp.bfloat16)
    return (attention_out, query_grads, key_grads, input_grads, weight_grads)
```

```python
import math

import jax
import jax.numpy as jnp
from jax import lax
from jax.experimental import pallas as pl
from jax.experimental.pallas import tpu as pltpu
from jax.sharding import PartitionSpec as P

HQ = 16
KVH = 4
HD = 128
CPR = 2
SPAN = 64
CHUNK = 256
GROUP = HQ // KVH
ROWS = SPAN * GROUP
INV_ROOT = 1.0 / math.sqrt(HD)
LOG2_SCALE = INV_ROOT * math.log2(math.e)
FAR = -1e30

NT = (((1,), (1,)), ((), ()))
TN = (((0,), (0,)), ((), ()))
NN = (((1,), (0,)), ((), ()))


def mm(a, b, dims):
    return lax.dot_general(a, b, dims, preferred_element_type=jnp.float32)


def attention_kernel(
    spans_ref,
    bounds_ref,
    q_ref,
    do_ref,
    kv_ref,
    start_ref,
    pos_ref,
    o_ref,
    dq_ref,
    dkv_ref,
    seq_ref,
    acc_ref,
    s_ref,
    p_ref,
    t_ref,
):
    num_spans = spans_ref.shape[0]
    kv_width = KVH * HD

    def to_sequence(i, _):
        src = pl.multiple_of(i * SPAN, SPAN)
        dst = pl.multiple_of(spans_ref[i] * SPAN, SPAN)
        seq_ref[pl.ds(dst, SPAN), :] = kv_ref[pl.ds(src, SPAN), :]
        acc_ref[pl.ds(src, SPAN), :] = jnp.zeros((SPAN, 2 * kv_width), jnp.float32)
        return 0

    lax.fori_loop(0, num_spans, to_sequence, 0)

    def rows_of(ref, span, head):
        return jnp.concatenate(
            [
                ref[
                    span * SPAN : (span + 1) * SPAN,
                    (head * GROUP + j) * HD : (head * GROUP + j + 1) * HD,
                ]
                for j in range(GROUP)
            ],
            axis=0,
        )

    def write_rows(ref, span, head, block):
        for j in range(GROUP):
            ref[
                span * SPAN : (span + 1) * SPAN,
                (head * GROUP + j) * HD : (head * GROUP + j + 1) * HD,
            ] = block[j * SPAN : (j + 1) * SPAN, :]

    def key_cols(head):
        return slice(head * HD, (head + 1) * HD)

    def value_cols(head):
        return slice(kv_width + head * HD, kv_width + (head + 1) * HD)

    for span in range(CPR):
        first = bounds_ref[2 * span]
        last = bounds_ref[2 * span + 1]
        start = start_ref[span : span + 1, :]
        pos = pos_ref[span : span + 1, :]

        def score_step(c, carry):
            rows = pl.ds(pl.multiple_of(c * CHUNK, CHUNK), CHUNK)
            key_pos = lax.broadcasted_iota(jnp.int32, (CHUNK, ROWS), 0) + c * CHUNK
            keep = (key_pos >= start) & (key_pos <= pos)
            out = []
            for head in range(KVH):
                top, total = carry[head]
                s = mm(seq_ref[rows, key_cols(head)], rows_of(q_ref, span, head), NT)
                s = jnp.where(keep, s * LOG2_SCALE, FAR)
                s_ref[head, c] = s
                new_top = jnp.maximum(top, jnp.max(s, axis=0, keepdims=True))
                new_total = total * jnp.exp2(top - new_top) + jnp.sum(
                    jnp.exp2(s - new_top), axis=0, keepdims=True
                )
                out.append((new_top, new_total))
            return tuple(out)

        empty = (jnp.full((1, ROWS), FAR, jnp.float32), jnp.zeros((1, ROWS), jnp.float32))
        stats = lax.fori_loop(first, last, score_step, (empty,) * KVH)
        log_total = [top + jnp.log2(total) for top, total in stats]
        t_ref[...] = jnp.zeros_like(t_ref)

        def value_step(c, _):
            rows = pl.ds(pl.multiple_of(c * CHUNK, CHUNK), CHUNK)
            for head in range(KVH):
                p = jnp.exp2(s_ref[head, c] - log_total[head]).astype(jnp.bfloat16)
                p_ref[head, c] = p
                t_ref[head] += mm(seq_ref[rows, value_cols(head)], p, TN)
                acc_ref[rows, value_cols(head)] += mm(p, rows_of(do_ref, span, head), NN)
            return 0

        lax.fori_loop(first, last, value_step, 0)
        delta = []
        for head in range(KVH):
            out_t = t_ref[head].astype(jnp.bfloat16).astype(jnp.float32)
            grad_t = rows_of(do_ref, span, head).astype(jnp.float32).T
            delta.append(jnp.sum(out_t * grad_t, axis=0, keepdims=True))
            write_rows(o_ref, span, head, out_t.T.astype(jnp.bfloat16))
        t_ref[...] = jnp.zeros_like(t_ref)

        def grad_step(c, _):
            rows = pl.ds(pl.multiple_of(c * CHUNK, CHUNK), CHUNK)
            for head in range(KVH):
                dp = mm(seq_ref[rows, value_cols(head)], rows_of(do_ref, span, head), NT)
                ds = (p_ref[head, c].astype(jnp.float32) * (dp - delta[head])).astype(jnp.bfloat16)
                t_ref[head] += mm(seq_ref[rows, key_cols(head)], ds, TN)
                acc_ref[rows, key_cols(head)] += mm(ds, rows_of(q_ref, span, head), NN)
            return 0

        lax.fori_loop(first, last, grad_step, 0)
        for head in range(KVH):
            write_rows(dq_ref, span, head, (t_ref[head] * INV_ROOT).T.astype(jnp.bfloat16))

    def to_layout(i, _):
        dst = pl.multiple_of(i * SPAN, SPAN)
        src = pl.multiple_of(spans_ref[i] * SPAN, SPAN)
        dkv_ref[pl.ds(dst, SPAN), 0:kv_width] = (
            acc_ref[pl.ds(src, SPAN), 0:kv_width] * INV_ROOT
        ).astype(jnp.bfloat16)
        dkv_ref[pl.ds(dst, SPAN), kv_width:] = acc_ref[pl.ds(src, SPAN), kv_width:].astype(
            jnp.bfloat16
        )
        return 0

    lax.fori_loop(0, num_spans, to_layout, 0)


def attention(queries, cotangent, kv_all, doc_list, span_list, rank_index):
    tokens, width = queries.shape
    seq_len, kv_width = kv_all.shape
    chunks = seq_len // CHUNK
    own_spans = lax.dynamic_slice_in_dim(span_list, rank_index * CPR, CPR)
    own_pos = own_spans[:, None] * SPAN + jnp.arange(SPAN, dtype=jnp.int32)[None, :]
    own_docs = doc_list.reshape(-1, SPAN)[own_spans]
    own_start = jnp.sum(
        (doc_list[None, None, :] < own_docs[:, :, None]).astype(jnp.int32), axis=2
    )
    first = own_start[:, 0] // CHUNK
    last = own_spans * SPAN // CHUNK + 1
    bounds = jnp.stack([first, last], axis=1).reshape(-1)
    vmem = pl.BlockSpec(memory_space=pltpu.VMEM)
    smem = pl.BlockSpec(memory_space=pltpu.SMEM)
    return pl.pallas_call(
        attention_kernel,
        out_shape=(
            jax.ShapeDtypeStruct((tokens, width), jnp.bfloat16),
            jax.ShapeDtypeStruct((tokens, width), jnp.bfloat16),
            jax.ShapeDtypeStruct((seq_len, kv_width), jnp.bfloat16),
        ),
        in_specs=[smem, smem, vmem, vmem, vmem, vmem, vmem],
        out_specs=(vmem, vmem, vmem),
        scratch_shapes=[
            pltpu.VMEM((seq_len, kv_width), jnp.bfloat16),
            pltpu.VMEM((seq_len, kv_width), jnp.float32),
            pltpu.VMEM((KVH, chunks, CHUNK, ROWS), jnp.float32),
            pltpu.VMEM((KVH, chunks, CHUNK, ROWS), jnp.bfloat16),
            pltpu.VMEM((KVH, HD, ROWS), jnp.float32),
        ],
        compiler_params=pltpu.CompilerParams(vmem_limit_bytes=52 * 1024 * 1024),
        cost_estimate=pl.CostEstimate(
            flops=12 * tokens * HQ * HD * seq_len // 2,
            bytes_accessed=8 * tokens * width + 4 * seq_len * kv_width,
            transcendentals=tokens * HQ * seq_len,
        ),
        name="attention",
    )(
        span_list,
        bounds,
        queries,
        cotangent,
        kv_all,
        jnp.tile(own_start, (1, GROUP)),
        jnp.tile(own_pos, (1, GROUP)),
    )


def per_device(hidden, queries, keys, cotangent, value_weight, doc_ids, span_order):
    kv_width = keys.shape[2]
    rank_index = lax.axis_index("ctx")
    token_rows = hidden[0]
    weight_all = lax.all_gather(value_weight, "ctx", axis=0, tiled=True)
    features = lax.all_to_all(token_rows, "ctx", split_axis=1, concat_axis=0, tiled=True)
    values_own = jnp.dot(
        token_rows, weight_all, preferred_element_type=jnp.float32
    ).astype(jnp.bfloat16)
    kv_all = lax.all_gather(
        jnp.concatenate([keys[0], values_own], axis=1), "ctx", axis=0, tiled=True
    )
    attention_out, query_grads, kv_terms = attention(
        queries[0], cotangent[0], kv_all, doc_ids[0], span_order[0], rank_index
    )
    kv_own = lax.psum_scatter(kv_terms, "ctx", scatter_dimension=0, tiled=True)
    key_own, value_own = kv_own[:, :kv_width], kv_own[:, kv_width:]
    value_all = lax.all_gather(value_own, "ctx", axis=0, tiled=True)
    input_grads = lax.dot_general(
        value_own, weight_all, NT, preferred_element_type=jnp.float32
    ).astype(jnp.bfloat16)
    weight_part = lax.dot_general(features, value_all, TN, preferred_element_type=jnp.float32)
    weight_total = lax.psum(weight_part.astype(jnp.bfloat16), "dp").astype(jnp.float32)
    weight_grads = (weight_total / lax.axis_size("dp")).astype(jnp.bfloat16)
    return (
        attention_out[None],
        query_grads[None],
        key_own[None],
        input_grads[None],
        weight_grads,
    )


def solution(mesh):
    return jax.shard_map(
        per_device,
        mesh=mesh,
        in_specs=(
            P("dp", "ctx", None),
            P("dp", "ctx", None),
            P("dp", "ctx", None),
            P("dp", "ctx", None),
            P("ctx", None),
            P("dp", None),
            P("dp", None),
        ),
        out_specs=(
            P("dp", "ctx", None),
            P("dp", "ctx", None),
            P("dp", "ctx", None),
            P("dp", "ctx", None),
            P("ctx", None),
        ),
        check_vma=False,
    )
```

```python
import functools
import math

import jax
import jax.numpy as jnp
from jax import lax
from jax.experimental import pallas as pl
from jax.experimental.pallas import tpu as pltpu
from jax.sharding import PartitionSpec as P

HQ = 16
KVH = 4
HD = 128
CPR = 2
SPAN = 64
CHUNK = 256
GROUP = HQ // KVH
ROWS = SPAN * GROUP
INV_ROOT = 1.0 / math.sqrt(HD)
LOG2_SCALE = INV_ROOT * math.log2(math.e)
FAR = -1e30
RING = 8
N_Z = 8
N_X = 4
STEPS = RING // 2
MESH = pl.DeviceIdType.MESH

NT = (((1,), (1,)), ((), ()))
TN = (((0,), (0,)), ((), ()))
NN = (((1,), (0,)), ((), ()))


def mm(a, b, dims):
    return lax.dot_general(a, b, dims, preferred_element_type=jnp.float32)


def attention_kernel(
    spans_ref,
    bounds_ref,
    q_ref,
    do_ref,
    k_ref,
    v_ref,
    start_ref,
    pos_ref,
    o_ref,
    dq_ref,
    dkv_ref,
    seq_ref,
    acc_ref,
    s_ref,
    p_ref,
    t_ref,
):
    num_spans = spans_ref.shape[0]
    kv_width = KVH * HD

    def to_sequence(i, _):
        src = pl.multiple_of(i * SPAN, SPAN)
        dst = pl.multiple_of(spans_ref[i] * SPAN, SPAN)
        seq_ref[pl.ds(dst, SPAN), 0:kv_width] = k_ref[pl.ds(src, SPAN), :]
        seq_ref[pl.ds(dst, SPAN), kv_width:] = v_ref[pl.ds(src, SPAN), :]
        acc_ref[pl.ds(src, SPAN), :] = jnp.zeros((SPAN, 2 * kv_width), jnp.float32)
        return 0

    lax.fori_loop(0, num_spans, to_sequence, 0)

    def rows_of(ref, span, head):
        return jnp.concatenate(
            [
                ref[
                    span * SPAN : (span + 1) * SPAN,
                    (head * GROUP + j) * HD : (head * GROUP + j + 1) * HD,
                ]
                for j in range(GROUP)
            ],
            axis=0,
        )

    def write_rows(ref, span, head, block):
        for j in range(GROUP):
            ref[
                span * SPAN : (span + 1) * SPAN,
                (head * GROUP + j) * HD : (head * GROUP + j + 1) * HD,
            ] = block[j * SPAN : (j + 1) * SPAN, :]

    def key_cols(head):
        return slice(head * HD, (head + 1) * HD)

    def value_cols(head):
        return slice(kv_width + head * HD, kv_width + (head + 1) * HD)

    for span in range(CPR):
        first = bounds_ref[2 * span]
        last = bounds_ref[2 * span + 1]
        start = start_ref[span : span + 1, :]
        pos = pos_ref[span : span + 1, :]

        def score_step(c, carry):
            rows = pl.ds(pl.multiple_of(c * CHUNK, CHUNK), CHUNK)
            key_pos = lax.broadcasted_iota(jnp.int32, (CHUNK, ROWS), 0) + c * CHUNK
            keep = (key_pos >= start) & (key_pos <= pos)
            out = []
            for head in range(KVH):
                top, total = carry[head]
                s = mm(seq_ref[rows, key_cols(head)], rows_of(q_ref, span, head), NT)
                s = jnp.where(keep, s * LOG2_SCALE, FAR)
                s_ref[head, c] = s
                new_top = jnp.maximum(top, jnp.max(s, axis=0, keepdims=True))
                new_total = total * jnp.exp2(top - new_top) + jnp.sum(
                    jnp.exp2(s - new_top), axis=0, keepdims=True
                )
                out.append((new_top, new_total))
            return tuple(out)

        empty = (jnp.full((1, ROWS), FAR, jnp.float32), jnp.zeros((1, ROWS), jnp.float32))
        stats = lax.fori_loop(first, last, score_step, (empty,) * KVH)
        log_total = [top + jnp.log2(total) for top, total in stats]
        t_ref[...] = jnp.zeros_like(t_ref)

        def value_step(c, _):
            rows = pl.ds(pl.multiple_of(c * CHUNK, CHUNK), CHUNK)
            for head in range(KVH):
                p = jnp.exp2(s_ref[head, c] - log_total[head]).astype(jnp.bfloat16)
                p_ref[head, c] = p
                t_ref[head] += mm(seq_ref[rows, value_cols(head)], p, TN)
                acc_ref[rows, value_cols(head)] += mm(p, rows_of(do_ref, span, head), NN)
            return 0

        lax.fori_loop(first, last, value_step, 0)
        delta = []
        for head in range(KVH):
            out_t = t_ref[head].astype(jnp.bfloat16).astype(jnp.float32)
            grad_t = rows_of(do_ref, span, head).astype(jnp.float32).T
            delta.append(jnp.sum(out_t * grad_t, axis=0, keepdims=True))
            write_rows(o_ref, span, head, out_t.T.astype(jnp.bfloat16))
        t_ref[...] = jnp.zeros_like(t_ref)

        def grad_step(c, _):
            rows = pl.ds(pl.multiple_of(c * CHUNK, CHUNK), CHUNK)
            for head in range(KVH):
                dp = mm(seq_ref[rows, value_cols(head)], rows_of(do_ref, span, head), NT)
                ds = (p_ref[head, c].astype(jnp.float32) * (dp - delta[head])).astype(jnp.bfloat16)
                t_ref[head] += mm(seq_ref[rows, key_cols(head)], ds, TN)
                acc_ref[rows, key_cols(head)] += mm(ds, rows_of(q_ref, span, head), NN)
            return 0

        lax.fori_loop(first, last, grad_step, 0)
        for head in range(KVH):
            write_rows(dq_ref, span, head, (t_ref[head] * INV_ROOT).T.astype(jnp.bfloat16))

    def to_layout(i, _):
        dst = pl.multiple_of(i * SPAN, SPAN)
        src = pl.multiple_of(spans_ref[i] * SPAN, SPAN)
        dkv_ref[pl.ds(dst, SPAN), 0:kv_width] = (
            acc_ref[pl.ds(src, SPAN), 0:kv_width] * INV_ROOT
        ).astype(jnp.bfloat16)
        dkv_ref[pl.ds(dst, SPAN), kv_width:] = acc_ref[pl.ds(src, SPAN), kv_width:].astype(
            jnp.bfloat16
        )
        return 0

    lax.fori_loop(0, num_spans, to_layout, 0)


def attention(queries, cotangent, k_all, v_all, doc_list, span_list, rank_index):
    tokens, width = queries.shape
    seq_len = k_all.shape[0]
    kv_width = 2 * k_all.shape[1]
    chunks = seq_len // CHUNK
    own_spans = lax.dynamic_slice_in_dim(span_list, rank_index * CPR, CPR)
    own_pos = own_spans[:, None] * SPAN + jnp.arange(SPAN, dtype=jnp.int32)[None, :]
    own_docs = doc_list.reshape(-1, SPAN)[own_spans]
    own_start = jnp.sum(
        (doc_list[None, None, :] < own_docs[:, :, None]).astype(jnp.int32), axis=2
    )
    first = own_start[:, 0] // CHUNK
    last = own_spans * SPAN // CHUNK + 1
    bounds = jnp.stack([first, last], axis=1).reshape(-1)
    vmem = pl.BlockSpec(memory_space=pltpu.VMEM)
    smem = pl.BlockSpec(memory_space=pltpu.SMEM)
    return pl.pallas_call(
        attention_kernel,
        out_shape=(
            jax.ShapeDtypeStruct((tokens, width), jnp.bfloat16),
            jax.ShapeDtypeStruct((tokens, width), jnp.bfloat16),
            jax.ShapeDtypeStruct((seq_len, kv_width), jnp.bfloat16),
        ),
        in_specs=[smem, smem, vmem, vmem, vmem, vmem, vmem, vmem],
        out_specs=(vmem, vmem, vmem),
        scratch_shapes=[
            pltpu.VMEM((seq_len, kv_width), jnp.bfloat16),
            pltpu.VMEM((seq_len, kv_width), jnp.float32),
            pltpu.VMEM((KVH, chunks, CHUNK, ROWS), jnp.float32),
            pltpu.VMEM((KVH, chunks, CHUNK, ROWS), jnp.bfloat16),
            pltpu.VMEM((KVH, HD, ROWS), jnp.float32),
        ],
        compiler_params=pltpu.CompilerParams(vmem_limit_bytes=52 * 1024 * 1024),
        cost_estimate=pl.CostEstimate(
            flops=12 * tokens * HQ * HD * seq_len // 2,
            bytes_accessed=8 * tokens * width + 4 * seq_len * kv_width,
            transcendentals=tokens * HQ * seq_len,
        ),
        name="attention",
    )(
        span_list,
        bounds,
        queries,
        cotangent,
        k_all,
        v_all,
        jnp.tile(own_start, (1, GROUP)),
        jnp.tile(own_pos, (1, GROUP)),
    )


def ring_place():
    me = lax.axis_index("ctx")
    y, core = me // 2, me % 2

    def at(chip, which):
        return {"ctx": lax.rem(chip + RING, RING) * 2 + which}

    return y, core, at(y + 1, core), at(y - 1, core), at(y, 1 - core)


def greet(partners):
    barrier = pltpu.get_barrier_semaphore()
    for partner in partners:
        pl.semaphore_signal(barrier, inc=1, device_id=partner, device_id_type=MESH)
    pl.semaphore_wait(barrier, len(partners))


def push(src, dst, send_sem, recv_sem, target):
    return pltpu.make_async_remote_copy(
        src_ref=src,
        dst_ref=dst,
        send_sem=send_sem,
        recv_sem=recv_sem,
        device_id=target,
        device_id_type=MESH,
    )


def carried(direction, step, half, short_step):
    return step != short_step or half == direction


def gather_kernel(count, *refs):
    in_refs, out_refs = refs[:count], refs[count : 2 * count]
    local_sem, ring_send, ring_recv, own_send, own_recv, sib_send, sib_recv = refs[2 * count :]
    y, core, right, left, sibling = ring_place()
    greet((right, left, sibling))

    def piece(a, chip, which, half):
        rows = in_refs[a].shape[0] // 2
        start = (lax.rem(chip + RING, RING) * 4 + which * 2 + half) * rows
        return out_refs[a].at[pl.ds(pl.multiple_of(start, rows), rows), :]

    def block(a, chip, which):
        rows = in_refs[a].shape[0]
        start = (lax.rem(chip + RING, RING) * 2 + which) * rows
        return out_refs[a].at[pl.ds(pl.multiple_of(start, rows), rows), :]

    sent = []
    local = []
    for a in range(count):
        half_rows = in_refs[a].shape[0] // 2
        for direction, target in ((0, right), (1, left)):
            for half in range(2):
                copy = push(
                    in_refs[a].at[pl.ds(half * half_rows, half_rows), :],
                    piece(a, y, core, half),
                    ring_send.at[a, direction, 0, half],
                    ring_recv.at[a, direction, 0, half],
                    target,
                )
                copy.start()
                sent.append(copy)
    for a in range(count):
        copy = push(in_refs[a], block(a, y, core), own_send.at[a], own_recv.at[a], sibling)
        copy.start()
        sent.append(copy)
        copy = pltpu.make_async_copy(in_refs[a], block(a, y, core), local_sem.at[a])
        copy.start()
        local.append(copy)
    for step in range(STEPS):
        for a in range(count):
            for half in range(2):
                for direction, target in ((0, right), (1, left)):
                    if not carried(direction, step, half, STEPS - 1):
                        continue
                    chip = y - 1 - step if direction == 0 else y + 1 + step
                    here = piece(a, chip, core, half)
                    push(
                        here,
                        here,
                        ring_send.at[a, direction, step, half],
                        ring_recv.at[a, direction, step, half],
                        target,
                    ).wait_recv()
                    if step + 1 < STEPS and carried(direction, step + 1, half, STEPS - 1):
                        copy = push(
                            here,
                            here,
                            ring_send.at[a, direction, step + 1, half],
                            ring_recv.at[a, direction, step + 1, half],
                            target,
                        )
                        copy.start()
                        sent.append(copy)
                    copy = push(
                        here,
                        here,
                        sib_send.at[a, direction, step, half],
                        sib_recv.at[a, direction, step, half],
                        sibling,
                    )
                    copy.start()
                    sent.append(copy)
    for a in range(count):
        there = block(a, y, 1 - core)
        push(there, there, own_send.at[a], own_recv.at[a], sibling).wait_recv()
        for step in range(STEPS):
            for half in range(2):
                for direction in range(2):
                    if not carried(direction, step, half, STEPS - 1):
                        continue
                    chip = y - 1 - step if direction == 0 else y + 1 + step
                    there = piece(a, chip, 1 - core, half)
                    push(
                        there,
                        there,
                        sib_send.at[a, direction, step, half],
                        sib_recv.at[a, direction, step, half],
                        sibling,
                    ).wait_recv()
    for copy in local:
        copy.wait()
    for copy in sent:
        copy.wait_send()


def gather(arrays, collective_id, name):
    count = len(arrays)
    ring = pltpu.SemaphoreType.DMA((count, 2, STEPS, 2))
    one = pltpu.SemaphoreType.DMA((count,))
    anywhere = pl.BlockSpec(memory_space=pl.ANY)
    total = sum(a.size for a in arrays) * 2 * RING
    return pl.pallas_call(
        functools.partial(gather_kernel, count),
        out_shape=tuple(
            jax.ShapeDtypeStruct((a.shape[0] * 2 * RING, a.shape[1]), a.dtype) for a in arrays
        ),
        in_specs=[anywhere] * count,
        out_specs=(anywhere,) * count,
        scratch_shapes=[one, ring, ring, one, one, ring, ring],
        compiler_params=pltpu.CompilerParams(collective_id=collective_id, has_side_effects=True),
        cost_estimate=pl.CostEstimate(flops=0, bytes_accessed=4 * total, transcendentals=0),
        name=name,
    )(*arrays)


NEAR = (4, 3, -3, 2, -2, 1, -1, 0)


def ring_reduce(x_ref, sib_ref, send_ref, recv_ref, sems, place, finish):
    sib_send, sib_recv, ring_send, ring_recv = sems
    y, core, right, left, sibling = place
    rows = sib_ref.shape[1]
    half_rows = rows // 2
    sent = []
    waited = set()

    def row_start(offset, which):
        return (lax.rem(y + offset + RING, RING) * 2 + which) * rows

    for i, offset in enumerate(NEAR):
        start = pl.multiple_of(row_start(offset, 1 - core), rows)
        copy = push(
            x_ref.at[pl.ds(start, rows), :],
            sib_ref.at[i],
            sib_send.at[i],
            sib_recv.at[i],
            sibling,
        )
        copy.start()
        sent.append(copy)

    def term(offset, half):
        i = NEAR.index(4 if offset == -4 else offset)
        if i not in waited:
            waited.add(i)
            push(
                sib_ref.at[i], sib_ref.at[i], sib_send.at[i], sib_recv.at[i], sibling
            ).wait_recv()
        start = pl.multiple_of(row_start(offset, core) + half * half_rows, half_rows)
        mine = x_ref[pl.ds(start, half_rows), :].astype(jnp.float32)
        theirs = sib_ref[i, half * half_rows : (half + 1) * half_rows, :]
        return mine + theirs.astype(jnp.float32)

    def arrived(direction, step, half):
        slot = recv_ref.at[direction, step, half]
        push(
            slot,
            slot,
            ring_send.at[direction, step, half],
            ring_recv.at[direction, step, half],
            right if direction == 0 else left,
        ).wait_recv()
        return recv_ref[direction, step, half].astype(jnp.float32)

    for step in range(STEPS):
        for half in range(2):
            for direction, target in ((0, right), (1, left)):
                if not carried(direction, step, half, 0):
                    continue
                distance = STEPS - step
                value = term(distance if direction == 0 else -distance, half)
                if step > 0 and carried(direction, step - 1, half, 0):
                    value = value + arrived(direction, step - 1, half)
                send_ref[direction, step, half] = value.astype(jnp.bfloat16)
                copy = push(
                    send_ref.at[direction, step, half],
                    recv_ref.at[direction, step, half],
                    ring_send.at[direction, step, half],
                    ring_recv.at[direction, step, half],
                    target,
                )
                copy.start()
                sent.append(copy)
    for half in range(2):
        value = term(0, half) + arrived(0, STEPS - 1, half) + arrived(1, STEPS - 1, half)
        finish(half, value)
    return sent


def ring_scratch(rows, cols):
    slots = pltpu.VMEM((2, STEPS, 2, rows // 2, cols), jnp.bfloat16)
    ring = pltpu.SemaphoreType.DMA((2, STEPS, 2))
    return [
        pltpu.VMEM((RING, rows, cols), jnp.bfloat16),
        slots,
        slots,
        pltpu.SemaphoreType.DMA((RING,)),
        pltpu.SemaphoreType.DMA((RING,)),
        ring,
        ring,
    ]


def scatter_kernel(x_ref, out_ref, sib_ref, send_ref, recv_ref, *sems):
    place = ring_place()
    greet(place[2:])
    half_rows = out_ref.shape[0] // 2

    def finish(half, value):
        out_ref[half * half_rows : (half + 1) * half_rows, :] = value.astype(jnp.bfloat16)

    for copy in ring_reduce(x_ref, sib_ref, send_ref, recv_ref, sems, place, finish):
        copy.wait_send()


def reduce_scatter(x, collective_id, name):
    rows, cols = x.shape[0] // (2 * RING), x.shape[1]
    vmem = pl.BlockSpec(memory_space=pltpu.VMEM)
    return pl.pallas_call(
        scatter_kernel,
        out_shape=jax.ShapeDtypeStruct((rows, cols), x.dtype),
        in_specs=[vmem],
        out_specs=vmem,
        scratch_shapes=ring_scratch(rows, cols),
        compiler_params=pltpu.CompilerParams(
            collective_id=collective_id,
            has_side_effects=True,
            vmem_limit_bytes=40 * 1024 * 1024,
        ),
        cost_estimate=pl.CostEstimate(
            flops=4 * x.size, bytes_accessed=4 * x.size, transcendentals=0
        ),
        name=name,
    )(x)


def weight_kernel(
    x_ref,
    out_ref,
    sib_ref,
    send_ref,
    recv_ref,
    sib_send,
    sib_recv,
    ring_send,
    ring_recv,
    own_ref,
    z_ref,
    part_ref,
    x_slots,
    total_ref,
    z_send,
    z_recv,
    x_send,
    x_recv,
    g_send,
    g_recv,
):
    place = ring_place()
    dp = lax.axis_index("dp")
    z, x = dp // N_X, dp % N_X
    z_after = [{"dp": lax.rem(z + k, N_Z) * N_X + x} for k in range(1, N_Z)]
    x_after = [{"dp": z * N_X + lax.rem(x + k, N_X)} for k in range(1, N_X)]
    greet(tuple(place[2:]) + tuple(z_after) + tuple(x_after))
    half_rows = own_ref.shape[0] // 2
    rows = own_ref.shape[0] // N_Z

    def finish(half, value):
        own_ref[half * half_rows : (half + 1) * half_rows, :] = value.astype(jnp.bfloat16)

    def z_rows(owner):
        return pl.ds(pl.multiple_of(lax.rem(owner + N_Z, N_Z) * rows, rows), rows)

    sems = (sib_send, sib_recv, ring_send, ring_recv)
    sent = ring_reduce(x_ref, sib_ref, send_ref, recv_ref, sems, place, finish)
    copies = [
        push(
            own_ref.at[z_rows(z + k), :],
            z_ref.at[k - 1],
            z_send.at[k - 1],
            z_recv.at[k - 1],
            z_after[k - 1],
        )
        for k in range(1, N_Z)
    ]
    for copy in copies:
        copy.start()
    sent += copies
    total = own_ref[z_rows(z), :].astype(jnp.float32)
    for k in range(1, N_Z):
        copies[k - 1].wait_recv()
        total = total + z_ref[k - 1].astype(jnp.float32)
    part_ref[...] = total.astype(jnp.bfloat16)
    x_slots[x] = part_ref[...]
    copies = [
        push(part_ref, x_slots.at[x], x_send.at[k - 1], x_recv.at[k - 1], x_after[k - 1])
        for k in range(1, N_X)
    ]
    for copy in copies:
        copy.start()
    sent += copies
    for k in range(1, N_X):
        slot = x_slots.at[lax.rem(x - k + N_X, N_X)]
        push(slot, slot, x_send.at[k - 1], x_recv.at[k - 1], x_after[k - 1]).wait_recv()
    total = x_slots[0].astype(jnp.float32)
    for k in range(1, N_X):
        total = total + x_slots[k].astype(jnp.float32)
    total_ref[z_rows(z), :] = (total * (1.0 / (N_Z * N_X))).astype(jnp.bfloat16)
    here = total_ref.at[z_rows(z), :]
    copies = [
        push(here, here, g_send.at[k - 1], g_recv.at[k - 1], z_after[k - 1])
        for k in range(1, N_Z)
    ]
    for copy in copies:
        copy.start()
    sent += copies
    for k in range(1, N_Z):
        there = total_ref.at[z_rows(z - k), :]
        push(there, there, g_send.at[k - 1], g_recv.at[k - 1], z_after[k - 1]).wait_recv()
    out_ref[...] = total_ref[...]
    for copy in sent:
        copy.wait_send()


def reduce_weights(x, collective_id, name):
    rows, cols = x.shape[0] // (2 * RING), x.shape[1]
    part = rows // N_Z
    vmem = pl.BlockSpec(memory_space=pltpu.VMEM)
    z_sem = pltpu.SemaphoreType.DMA((N_Z - 1,))
    x_sem = pltpu.SemaphoreType.DMA((N_X - 1,))
    return pl.pallas_call(
        weight_kernel,
        out_shape=jax.ShapeDtypeStruct((rows, cols), x.dtype),
        in_specs=[vmem],
        out_specs=vmem,
        scratch_shapes=ring_scratch(rows, cols)
        + [
            pltpu.VMEM((rows, cols), jnp.bfloat16),
            pltpu.VMEM((N_Z - 1, part, cols), jnp.bfloat16),
            pltpu.VMEM((part, cols), jnp.bfloat16),
            pltpu.VMEM((N_X, part, cols), jnp.bfloat16),
            pltpu.VMEM((rows, cols), jnp.bfloat16),
            z_sem,
            z_sem,
            x_sem,
            x_sem,
            z_sem,
            z_sem,
        ],
        compiler_params=pltpu.CompilerParams(
            collective_id=collective_id,
            has_side_effects=True,
            vmem_limit_bytes=40 * 1024 * 1024,
        ),
        cost_estimate=pl.CostEstimate(
            flops=4 * x.size, bytes_accessed=4 * x.size, transcendentals=0
        ),
        name=name,
    )(x)


def per_device(hidden, queries, keys, cotangent, value_weight, doc_ids, span_order):
    kv_width = keys.shape[2]
    rank_index = lax.axis_index("ctx")
    token_rows = hidden[0]
    weight_all, key_all = gather((value_weight, keys[0]), 0, "gather_weight_keys")
    values_own = jnp.dot(
        token_rows, weight_all, preferred_element_type=jnp.float32
    ).astype(jnp.bfloat16)
    (value_all,) = gather((values_own,), 1, "gather_values")
    attention_out, query_grads, kv_terms = attention(
        queries[0], cotangent[0], key_all, value_all, doc_ids[0], span_order[0], rank_index
    )
    kv_own = reduce_scatter(kv_terms, 2, "scatter_terms")
    key_own, value_own = kv_own[:, :kv_width], kv_own[:, kv_width:]
    weight_part = lax.dot_general(
        token_rows, value_own, TN, preferred_element_type=jnp.float32
    ).astype(jnp.bfloat16)
    weight_grads = reduce_weights(weight_part, 3, "reduce_weights")
    input_grads = lax.dot_general(
        value_own, weight_all, NT, preferred_element_type=jnp.float32
    ).astype(jnp.bfloat16)
    return (
        attention_out[None],
        query_grads[None],
        key_own[None],
        input_grads[None],
        weight_grads,
    )


def solution(mesh):
    return jax.shard_map(
        per_device,
        mesh=mesh,
        in_specs=(
            P("dp", "ctx", None),
            P("dp", "ctx", None),
            P("dp", "ctx", None),
            P("dp", "ctx", None),
            P("ctx", None),
            P("dp", None),
            P("dp", None),
        ),
        out_specs=(
            P("dp", "ctx", None),
            P("dp", "ctx", None),
            P("dp", "ctx", None),
            P("dp", "ctx", None),
            P("ctx", None),
        ),
        check_vma=False,
    )
```

```python
import functools
import math

import jax
import jax.numpy as jnp
from jax import lax
from jax.experimental import pallas as pl
from jax.experimental.pallas import tpu as pltpu
from jax.sharding import PartitionSpec as P

HQ = 16
KVH = 4
HD = 128
CPR = 2
SPAN = 64
CHUNK = 256
GROUP = HQ // KVH
ROWS = SPAN * GROUP
INV_ROOT = 1.0 / math.sqrt(HD)
LOG2_SCALE = INV_ROOT * math.log2(math.e)
FAR = -1e30
RING = 8
N_Z = 8
N_X = 4
STEPS = RING // 2
MESH = pl.DeviceIdType.MESH

NT = (((1,), (1,)), ((), ()))
TN = (((0,), (0,)), ((), ()))
NN = (((1,), (0,)), ((), ()))


def mm(a, b, dims):
    return lax.dot_general(a, b, dims, preferred_element_type=jnp.float32)


def attention_kernel(
    spans_ref,
    rank_ref,
    docs_ref,
    q_ref,
    do_ref,
    k_ref,
    v_ref,
    o_ref,
    dq_ref,
    dkv_ref,
    seq_ref,
    acc_ref,
    s_ref,
    p_ref,
    t_ref,
):
    num_spans = spans_ref.shape[0]
    kv_width = KVH * HD

    def to_sequence(i, _):
        src = pl.multiple_of(i * SPAN, SPAN)
        dst = pl.multiple_of(spans_ref[i] * SPAN, SPAN)
        seq_ref[pl.ds(dst, SPAN), 0:kv_width] = k_ref[pl.ds(src, SPAN), :]
        seq_ref[pl.ds(dst, SPAN), kv_width:] = v_ref[pl.ds(src, SPAN), :]
        acc_ref[pl.ds(src, SPAN), :] = jnp.zeros((SPAN, 2 * kv_width), jnp.float32)
        return 0

    lax.fori_loop(0, num_spans, to_sequence, 0)

    def rows_of(ref, span, head):
        return jnp.concatenate(
            [
                ref[
                    span * SPAN : (span + 1) * SPAN,
                    (head * GROUP + j) * HD : (head * GROUP + j + 1) * HD,
                ]
                for j in range(GROUP)
            ],
            axis=0,
        )

    def write_rows(ref, span, head, block):
        for j in range(GROUP):
            ref[
                span * SPAN : (span + 1) * SPAN,
                (head * GROUP + j) * HD : (head * GROUP + j + 1) * HD,
            ] = block[j * SPAN : (j + 1) * SPAN, :]

    def key_cols(head):
        return slice(head * HD, (head + 1) * HD)

    def value_cols(head):
        return slice(kv_width + head * HD, kv_width + (head + 1) * HD)

    def first_with(doc, low, high, rounds):
        def halve(_, ends):
            low, high = ends
            mid = (low + high) // 2
            below = docs_ref[mid] < doc
            return jnp.where(below, mid + 1, low), jnp.where(below, high, mid)

        return lax.fori_loop(0, rounds, halve, (low, high))[1]

    for span in range(CPR):
        begin = spans_ref[rank_ref[0] * CPR + span] * SPAN
        doc_low = docs_ref[begin]
        doc_high = docs_ref[begin + SPAN - 1]
        pos = begin + lax.broadcasted_iota(jnp.int32, (1, ROWS), 1) % SPAN
        lowest = first_with(doc_low, 0, begin, 11)
        first = lowest // CHUNK
        last = begin // CHUNK + 1

        def next_doc(doc, start):
            bound = first_with(doc, begin, begin + SPAN - 1, 6)
            return jnp.where(pos >= bound, bound, start)

        start = lax.fori_loop(
            doc_low + 1, doc_high + 1, next_doc, jnp.full((1, ROWS), lowest, jnp.int32)
        )

        def score_step(c, carry):
            rows = pl.ds(pl.multiple_of(c * CHUNK, CHUNK), CHUNK)
            key_pos = lax.broadcasted_iota(jnp.int32, (CHUNK, ROWS), 0) + c * CHUNK
            keep = (key_pos >= start) & (key_pos <= pos)
            out = []
            for head in range(KVH):
                top, total = carry[head]
                s = mm(seq_ref[rows, key_cols(head)], rows_of(q_ref, span, head), NT)
                s = jnp.where(keep, s * LOG2_SCALE, FAR)
                s_ref[head, c] = s
                new_top = jnp.maximum(top, jnp.max(s, axis=0, keepdims=True))
                new_total = total * jnp.exp2(top - new_top) + jnp.sum(
                    jnp.exp2(s - new_top), axis=0, keepdims=True
                )
                out.append((new_top, new_total))
            return tuple(out)

        empty = (jnp.full((1, ROWS), FAR, jnp.float32), jnp.zeros((1, ROWS), jnp.float32))
        stats = lax.fori_loop(first, last, score_step, (empty,) * KVH)
        log_total = [top + jnp.log2(total) for top, total in stats]
        t_ref[...] = jnp.zeros_like(t_ref)

        def value_step(c, _):
            rows = pl.ds(pl.multiple_of(c * CHUNK, CHUNK), CHUNK)
            for head in range(KVH):
                p = jnp.exp2(s_ref[head, c] - log_total[head]).astype(jnp.bfloat16)
                p_ref[head, c] = p
                t_ref[head] += mm(seq_ref[rows, value_cols(head)], p, TN)
                acc_ref[rows, value_cols(head)] += mm(p, rows_of(do_ref, span, head), NN)
            return 0

        lax.fori_loop(first, last, value_step, 0)
        delta = []
        for head in range(KVH):
            out_t = t_ref[head].astype(jnp.bfloat16).astype(jnp.float32)
            grad_t = rows_of(do_ref, span, head).astype(jnp.float32).T
            delta.append(jnp.sum(out_t * grad_t, axis=0, keepdims=True))
            write_rows(o_ref, span, head, out_t.T.astype(jnp.bfloat16))
        t_ref[...] = jnp.zeros_like(t_ref)

        def grad_step(c, _):
            rows = pl.ds(pl.multiple_of(c * CHUNK, CHUNK), CHUNK)
            for head in range(KVH):
                dp = mm(seq_ref[rows, value_cols(head)], rows_of(do_ref, span, head), NT)
                ds = (p_ref[head, c].astype(jnp.float32) * (dp - delta[head])).astype(jnp.bfloat16)
                t_ref[head] += mm(seq_ref[rows, key_cols(head)], ds, TN)
                acc_ref[rows, key_cols(head)] += mm(ds, rows_of(q_ref, span, head), NN)
            return 0

        lax.fori_loop(first, last, grad_step, 0)
        for head in range(KVH):
            write_rows(dq_ref, span, head, (t_ref[head] * INV_ROOT).T.astype(jnp.bfloat16))

    def to_layout(i, _):
        dst = pl.multiple_of(i * SPAN, SPAN)
        src = pl.multiple_of(spans_ref[i] * SPAN, SPAN)
        dkv_ref[pl.ds(dst, SPAN), 0:kv_width] = (
            acc_ref[pl.ds(src, SPAN), 0:kv_width] * INV_ROOT
        ).astype(jnp.bfloat16)
        dkv_ref[pl.ds(dst, SPAN), kv_width:] = acc_ref[pl.ds(src, SPAN), kv_width:].astype(
            jnp.bfloat16
        )
        return 0

    lax.fori_loop(0, num_spans, to_layout, 0)


def attention(queries, cotangent, k_all, v_all, doc_list, span_list, rank_index):
    tokens, width = queries.shape
    seq_len = k_all.shape[0]
    kv_width = 2 * k_all.shape[1]
    chunks = seq_len // CHUNK
    vmem = pl.BlockSpec(memory_space=pltpu.VMEM)
    smem = pl.BlockSpec(memory_space=pltpu.SMEM)
    return pl.pallas_call(
        attention_kernel,
        out_shape=(
            jax.ShapeDtypeStruct((tokens, width), jnp.bfloat16),
            jax.ShapeDtypeStruct((tokens, width), jnp.bfloat16),
            jax.ShapeDtypeStruct((seq_len, kv_width), jnp.bfloat16),
        ),
        in_specs=[smem, smem, smem, vmem, vmem, vmem, vmem],
        out_specs=(vmem, vmem, vmem),
        scratch_shapes=[
            pltpu.VMEM((seq_len, kv_width), jnp.bfloat16),
            pltpu.VMEM((seq_len, kv_width), jnp.float32),
            pltpu.VMEM((KVH, chunks, CHUNK, ROWS), jnp.float32),
            pltpu.VMEM((KVH, chunks, CHUNK, ROWS), jnp.bfloat16),
            pltpu.VMEM((KVH, HD, ROWS), jnp.float32),
        ],
        compiler_params=pltpu.CompilerParams(vmem_limit_bytes=52 * 1024 * 1024),
        cost_estimate=pl.CostEstimate(
            flops=12 * tokens * HQ * HD * seq_len // 2,
            bytes_accessed=8 * tokens * width + 4 * seq_len * kv_width,
            transcendentals=tokens * HQ * seq_len,
        ),
        name="attention",
    )(
        span_list,
        jnp.reshape(rank_index, (1,)),
        doc_list,
        queries,
        cotangent,
        k_all,
        v_all,
    )


def ring_place():
    me = lax.axis_index("ctx")
    y, core = me // 2, me % 2

    def at(chip, which):
        return {"ctx": lax.rem(chip + RING, RING) * 2 + which}

    return y, core, at(y + 1, core), at(y - 1, core), at(y, 1 - core)


def greet(partners):
    barrier = pltpu.get_barrier_semaphore()
    for partner in partners:
        pl.semaphore_signal(barrier, inc=1, device_id=partner, device_id_type=MESH)
    pl.semaphore_wait(barrier, len(partners))


def push(src, dst, send_sem, recv_sem, target):
    return pltpu.make_async_remote_copy(
        src_ref=src,
        dst_ref=dst,
        send_sem=send_sem,
        recv_sem=recv_sem,
        device_id=target,
        device_id_type=MESH,
    )


def carried(direction, step, half, short_step):
    return step != short_step or half == direction


class RingGather:
    def __init__(self, a, own_ref, all_ref, sems, place):
        self.a, self.own_ref, self.all_ref = a, own_ref, all_ref
        self.rows = own_ref.shape[0]
        (
            self.local_sem,
            self.ring_send,
            self.ring_recv,
            self.own_send,
            self.own_recv,
            self.sib_send,
            self.sib_recv,
        ) = sems
        self.y, self.core, self.right, self.left, self.sibling = place
        self.sent = []

    def piece(self, chip, which, half):
        rows = self.rows // 2
        start = (lax.rem(chip + RING, RING) * 4 + which * 2 + half) * rows
        return self.all_ref.at[pl.ds(pl.multiple_of(start, rows), rows), :]

    def block(self, chip, which):
        start = (lax.rem(chip + RING, RING) * 2 + which) * self.rows
        return self.all_ref.at[pl.ds(pl.multiple_of(start, self.rows), self.rows), :]

    def send(self, copy):
        copy.start()
        self.sent.append(copy)

    def along(self, src, dst, direction, step, half):
        return push(
            src,
            dst,
            self.ring_send.at[self.a, direction, step, half],
            self.ring_recv.at[self.a, direction, step, half],
            self.left if direction else self.right,
        )

    def across(self, ref, direction, step, half):
        return push(
            ref,
            ref,
            self.sib_send.at[self.a, direction, step, half],
            self.sib_recv.at[self.a, direction, step, half],
            self.sibling,
        )

    def own_across(self, src, dst):
        return push(src, dst, self.own_send.at[self.a], self.own_recv.at[self.a], self.sibling)

    def start(self):
        rows = self.rows // 2
        for half in range(2):
            for direction in range(2):
                src = self.own_ref.at[pl.ds(half * rows, rows), :]
                dst = self.piece(self.y, self.core, half)
                self.send(self.along(src, dst, direction, 0, half))
        mine = self.block(self.y, self.core)
        self.send(self.own_across(self.own_ref, mine))
        self.local = pltpu.make_async_copy(self.own_ref, mine, self.local_sem.at[self.a])
        self.local.start()

    def pieces(self, step):
        for half in range(2):
            for direction in range(2):
                if carried(direction, step, half, STEPS - 1):
                    chip = self.y + 1 + step if direction else self.y - 1 - step
                    yield direction, half, chip

    def step(self, step):
        for direction, half, chip in self.pieces(step):
            here = self.piece(chip, self.core, half)
            self.along(here, here, direction, step, half).wait_recv()
            if step + 1 < STEPS and carried(direction, step + 1, half, STEPS - 1):
                self.send(self.along(here, here, direction, step + 1, half))
            self.send(self.across(here, direction, step, half))

    def own_from_sibling(self):
        there = self.block(self.y, 1 - self.core)
        self.own_across(there, there).wait_recv()

    def from_sibling(self, step):
        for direction, half, chip in self.pieces(step):
            there = self.piece(chip, 1 - self.core, half)
            self.across(there, direction, step, half).wait_recv()

    def finish(self):
        self.local.wait()
        for copy in self.sent:
            copy.wait_send()


def front_kernel(
    hidden_ref,
    weight_ref,
    keys_ref,
    weight_out,
    key_out,
    value_out,
    weight_all,
    acc_ref,
    values_ref,
    out_sem,
    *sems,
):
    place = ring_place()
    y, core = place[:2]
    greet(place[2:])
    weight = RingGather(0, weight_ref, weight_all, sems, place)
    key = RingGather(1, keys_ref, key_out, sems, place)
    value = RingGather(2, values_ref, value_out, sems, place)
    depth = weight_ref.shape[0]

    def project(chip, which):
        start = (lax.rem(chip + RING, RING) * 2 + which) * depth
        rows = pl.ds(pl.multiple_of(start, depth), depth)
        acc_ref[...] += mm(hidden_ref[:, rows], weight_all[rows, :], NN)

    weight.start()
    acc_ref[...] = jnp.zeros_like(acc_ref)
    for step in range(STEPS):
        weight.step(step)
        if step == STEPS - 2:
            key.start()
        if step == 0:
            weight.local.wait()
            project(y, core)
            weight.own_from_sibling()
            project(y, 1 - core)
        else:
            weight.from_sibling(step - 1)
            project(y - step, 1 - core)
            project(y + step, 1 - core)
        project(y - 1 - step, core)
        if step < STEPS - 1:
            project(y + 1 + step, core)
    weight.from_sibling(STEPS - 1)
    project(y + STEPS, 1 - core)
    values_ref[...] = acc_ref[...].astype(jnp.bfloat16)
    value.start()
    keep = pltpu.make_async_copy(weight_all, weight_out, out_sem)
    keep.start()
    for step in range(STEPS):
        key.step(step)
        value.step(step)
    for each in (key, value):
        each.own_from_sibling()
        for step in range(STEPS):
            each.from_sibling(step)
    keep.wait()
    for each in (key, value):
        each.finish()
    for copy in weight.sent:
        copy.wait_send()


def front(hidden, value_weight, keys, collective_id):
    tokens, kv_width = keys.shape
    ring = pltpu.SemaphoreType.DMA((3, 2, STEPS, 2))
    one = pltpu.SemaphoreType.DMA((3,))
    anywhere = pl.BlockSpec(memory_space=pl.ANY)
    vmem = pl.BlockSpec(memory_space=pltpu.VMEM)
    depth = value_weight.shape[0] * 2 * RING
    gathered = jax.ShapeDtypeStruct((tokens * 2 * RING, kv_width), keys.dtype)
    return pl.pallas_call(
        front_kernel,
        out_shape=(
            jax.ShapeDtypeStruct((depth, kv_width), value_weight.dtype),
            gathered,
            gathered,
        ),
        in_specs=[vmem, vmem, vmem],
        out_specs=(anywhere,) * 3,
        scratch_shapes=[
            pltpu.VMEM((depth, kv_width), jnp.bfloat16),
            pltpu.VMEM((tokens, kv_width), jnp.float32),
            pltpu.VMEM((tokens, kv_width), jnp.bfloat16),
            pltpu.SemaphoreType.DMA,
            one,
            ring,
            ring,
            one,
            one,
            ring,
            ring,
        ],
        compiler_params=pltpu.CompilerParams(
            collective_id=collective_id,
            has_side_effects=True,
            vmem_limit_bytes=24 * 1024 * 1024,
        ),
        cost_estimate=pl.CostEstimate(
            flops=2 * tokens * depth * kv_width,
            bytes_accessed=4 * depth * kv_width,
            transcendentals=0,
        ),
        name="front",
    )(hidden, value_weight, keys)


NEAR = (4, 3, -3, 2, -2, 1, -1, 0)


def ring_reduce(x_ref, sib_ref, send_ref, recv_ref, sems, place, finish):
    sib_send, sib_recv, ring_send, ring_recv = sems
    y, core, right, left, sibling = place
    rows = sib_ref.shape[1]
    half_rows = rows // 2
    sent = []
    waited = set()

    def row_start(offset, which):
        return (lax.rem(y + offset + RING, RING) * 2 + which) * rows

    for i, offset in enumerate(NEAR):
        start = pl.multiple_of(row_start(offset, 1 - core), rows)
        copy = push(
            x_ref.at[pl.ds(start, rows), :],
            sib_ref.at[i],
            sib_send.at[i],
            sib_recv.at[i],
            sibling,
        )
        copy.start()
        sent.append(copy)

    def term(offset, half):
        i = NEAR.index(4 if offset == -4 else offset)
        if i not in waited:
            waited.add(i)
            push(
                sib_ref.at[i], sib_ref.at[i], sib_send.at[i], sib_recv.at[i], sibling
            ).wait_recv()
        start = pl.multiple_of(row_start(offset, core) + half * half_rows, half_rows)
        mine = x_ref[pl.ds(start, half_rows), :].astype(jnp.float32)
        theirs = sib_ref[i, half * half_rows : (half + 1) * half_rows, :]
        return mine + theirs.astype(jnp.float32)

    def arrived(direction, step, half):
        slot = recv_ref.at[direction, step, half]
        push(
            slot,
            slot,
            ring_send.at[direction, step, half],
            ring_recv.at[direction, step, half],
            right if direction == 0 else left,
        ).wait_recv()
        return recv_ref[direction, step, half].astype(jnp.float32)

    for step in range(STEPS):
        for half in range(2):
            for direction, target in ((0, right), (1, left)):
                if not carried(direction, step, half, 0):
                    continue
                distance = STEPS - step
                value = term(distance if direction == 0 else -distance, half)
                if step > 0 and carried(direction, step - 1, half, 0):
                    value = value + arrived(direction, step - 1, half)
                send_ref[direction, step, half] = value.astype(jnp.bfloat16)
                copy = push(
                    send_ref.at[direction, step, half],
                    recv_ref.at[direction, step, half],
                    ring_send.at[direction, step, half],
                    ring_recv.at[direction, step, half],
                    target,
                )
                copy.start()
                sent.append(copy)
    for half in range(2):
        value = term(0, half) + arrived(0, STEPS - 1, half) + arrived(1, STEPS - 1, half)
        finish(half, value)
    return sent


def ring_scratch(rows, cols):
    slots = pltpu.VMEM((2, STEPS, 2, rows // 2, cols), jnp.bfloat16)
    ring = pltpu.SemaphoreType.DMA((2, STEPS, 2))
    return [
        pltpu.VMEM((RING, rows, cols), jnp.bfloat16),
        slots,
        slots,
        pltpu.SemaphoreType.DMA((RING,)),
        pltpu.SemaphoreType.DMA((RING,)),
        ring,
        ring,
    ]


def scatter_kernel(x_ref, out_ref, sib_ref, send_ref, recv_ref, *sems):
    place = ring_place()
    greet(place[2:])
    half_rows = out_ref.shape[0] // 2

    def finish(half, value):
        out_ref[half * half_rows : (half + 1) * half_rows, :] = value.astype(jnp.bfloat16)

    for copy in ring_reduce(x_ref, sib_ref, send_ref, recv_ref, sems, place, finish):
        copy.wait_send()


def reduce_scatter(x, collective_id, name):
    rows, cols = x.shape[0] // (2 * RING), x.shape[1]
    vmem = pl.BlockSpec(memory_space=pltpu.VMEM)
    return pl.pallas_call(
        scatter_kernel,
        out_shape=jax.ShapeDtypeStruct((rows, cols), x.dtype),
        in_specs=[vmem],
        out_specs=vmem,
        scratch_shapes=ring_scratch(rows, cols),
        compiler_params=pltpu.CompilerParams(
            collective_id=collective_id,
            has_side_effects=True,
            vmem_limit_bytes=40 * 1024 * 1024,
        ),
        cost_estimate=pl.CostEstimate(
            flops=4 * x.size, bytes_accessed=4 * x.size, transcendentals=0
        ),
        name=name,
    )(x)


def weight_kernel(
    x_ref,
    out_ref,
    sib_ref,
    send_ref,
    recv_ref,
    sib_send,
    sib_recv,
    ring_send,
    ring_recv,
    own_ref,
    z_ref,
    part_ref,
    x_slots,
    total_ref,
    z_send,
    z_recv,
    x_send,
    x_recv,
    g_send,
    g_recv,
):
    place = ring_place()
    dp = lax.axis_index("dp")
    z, x = dp // N_X, dp % N_X
    z_after = [{"dp": lax.rem(z + k, N_Z) * N_X + x} for k in range(1, N_Z)]
    x_after = [{"dp": z * N_X + lax.rem(x + k, N_X)} for k in range(1, N_X)]
    greet(tuple(place[2:]) + tuple(z_after) + tuple(x_after))
    half_rows = own_ref.shape[0] // 2
    rows = own_ref.shape[0] // N_Z

    def finish(half, value):
        own_ref[half * half_rows : (half + 1) * half_rows, :] = value.astype(jnp.bfloat16)

    def z_rows(owner):
        return pl.ds(pl.multiple_of(lax.rem(owner + N_Z, N_Z) * rows, rows), rows)

    sems = (sib_send, sib_recv, ring_send, ring_recv)
    sent = ring_reduce(x_ref, sib_ref, send_ref, recv_ref, sems, place, finish)
    copies = [
        push(
            own_ref.at[z_rows(z + k), :],
            z_ref.at[k - 1],
            z_send.at[k - 1],
            z_recv.at[k - 1],
            z_after[k - 1],
        )
        for k in range(1, N_Z)
    ]
    for copy in copies:
        copy.start()
    sent += copies
    total = own_ref[z_rows(z), :].astype(jnp.float32)
    for k in range(1, N_Z):
        copies[k - 1].wait_recv()
        total = total + z_ref[k - 1].astype(jnp.float32)
    part_ref[...] = total.astype(jnp.bfloat16)
    x_slots[x] = part_ref[...]
    copies = [
        push(part_ref, x_slots.at[x], x_send.at[k - 1], x_recv.at[k - 1], x_after[k - 1])
        for k in range(1, N_X)
    ]
    for copy in copies:
        copy.start()
    sent += copies
    for k in range(1, N_X):
        slot = x_slots.at[lax.rem(x - k + N_X, N_X)]
        push(slot, slot, x_send.at[k - 1], x_recv.at[k - 1], x_after[k - 1]).wait_recv()
    total = x_slots[0].astype(jnp.float32)
    for k in range(1, N_X):
        total = total + x_slots[k].astype(jnp.float32)
    total_ref[z_rows(z), :] = (total * (1.0 / (N_Z * N_X))).astype(jnp.bfloat16)
    here = total_ref.at[z_rows(z), :]
    copies = [
        push(here, here, g_send.at[k - 1], g_recv.at[k - 1], z_after[k - 1])
        for k in range(1, N_Z)
    ]
    for copy in copies:
        copy.start()
    sent += copies
    for k in range(1, N_Z):
        there = total_ref.at[z_rows(z - k), :]
        push(there, there, g_send.at[k - 1], g_recv.at[k - 1], z_after[k - 1]).wait_recv()
    out_ref[...] = total_ref[...]
    for copy in sent:
        copy.wait_send()


def reduce_weights(x, collective_id, name):
    rows, cols = x.shape[0] // (2 * RING), x.shape[1]
    part = rows // N_Z
    vmem = pl.BlockSpec(memory_space=pltpu.VMEM)
    z_sem = pltpu.SemaphoreType.DMA((N_Z - 1,))
    x_sem = pltpu.SemaphoreType.DMA((N_X - 1,))
    return pl.pallas_call(
        weight_kernel,
        out_shape=jax.ShapeDtypeStruct((rows, cols), x.dtype),
        in_specs=[vmem],
        out_specs=vmem,
        scratch_shapes=ring_scratch(rows, cols)
        + [
            pltpu.VMEM((rows, cols), jnp.bfloat16),
            pltpu.VMEM((N_Z - 1, part, cols), jnp.bfloat16),
            pltpu.VMEM((part, cols), jnp.bfloat16),
            pltpu.VMEM((N_X, part, cols), jnp.bfloat16),
            pltpu.VMEM((rows, cols), jnp.bfloat16),
            z_sem,
            z_sem,
            x_sem,
            x_sem,
            z_sem,
            z_sem,
        ],
        compiler_params=pltpu.CompilerParams(
            collective_id=collective_id,
            has_side_effects=True,
            vmem_limit_bytes=40 * 1024 * 1024,
        ),
        cost_estimate=pl.CostEstimate(
            flops=4 * x.size, bytes_accessed=4 * x.size, transcendentals=0
        ),
        name=name,
    )(x)


def per_device(hidden, queries, keys, cotangent, value_weight, doc_ids, span_order):
    kv_width = keys.shape[2]
    rank_index = lax.axis_index("ctx")
    token_rows = hidden[0]
    weight_all, key_all, value_all = front(token_rows, value_weight, keys[0], 0)
    attention_out, query_grads, kv_terms = attention(
        queries[0], cotangent[0], key_all, value_all, doc_ids[0], span_order[0], rank_index
    )
    kv_own = reduce_scatter(kv_terms, 2, "scatter_terms")
    key_own, value_own = kv_own[:, :kv_width], kv_own[:, kv_width:]
    weight_part = lax.dot_general(
        token_rows, value_own, TN, preferred_element_type=jnp.float32
    ).astype(jnp.bfloat16)
    weight_grads = reduce_weights(weight_part, 3, "reduce_weights")
    input_grads = lax.dot_general(
        value_own, weight_all, NT, preferred_element_type=jnp.float32
    ).astype(jnp.bfloat16)
    return (
        attention_out[None],
        query_grads[None],
        key_own[None],
        input_grads[None],
        weight_grads,
    )


def solution(mesh):
    return jax.shard_map(
        per_device,
        mesh=mesh,
        in_specs=(
            P("dp", "ctx", None),
            P("dp", "ctx", None),
            P("dp", "ctx", None),
            P("dp", "ctx", None),
            P("ctx", None),
            P("dp", None),
            P("dp", None),
        ),
        out_specs=(
            P("dp", "ctx", None),
            P("dp", "ctx", None),
            P("dp", "ctx", None),
            P("dp", "ctx", None),
            P("ctx", None),
        ),
        check_vma=False,
    )
```

```python
import functools
import math

import jax
import jax.numpy as jnp
from jax import lax
from jax.experimental import pallas as pl
from jax.experimental.pallas import tpu as pltpu
from jax.sharding import PartitionSpec as P

HQ = 16
KVH = 4
HD = 128
CPR = 2
SPAN = 64
CHUNK = 256
GROUP = HQ // KVH
ROWS = SPAN * GROUP
INV_ROOT = 1.0 / math.sqrt(HD)
LOG2_SCALE = INV_ROOT * math.log2(math.e)
FAR = -1e30
RING = 8
N_Z = 8
N_X = 4
STEPS = RING // 2
MESH = pl.DeviceIdType.MESH

NT = (((1,), (1,)), ((), ()))
TN = (((0,), (0,)), ((), ()))
NN = (((1,), (0,)), ((), ()))


def mm(a, b, dims):
    return lax.dot_general(a, b, dims, preferred_element_type=jnp.float32)


def attention_kernel(
    spans_ref,
    rank_ref,
    docs_ref,
    q_ref,
    do_ref,
    k_ref,
    v_ref,
    o_ref,
    dq_ref,
    dkv_ref,
    seq_ref,
    acc_ref,
    s_ref,
    p_ref,
    t_ref,
):
    num_spans = spans_ref.shape[0]
    kv_width = KVH * HD

    def to_sequence(i, _):
        src = pl.multiple_of(i * SPAN, SPAN)
        dst = pl.multiple_of(spans_ref[i] * SPAN, SPAN)
        seq_ref[pl.ds(dst, SPAN), 0:kv_width] = k_ref[pl.ds(src, SPAN), :]
        seq_ref[pl.ds(dst, SPAN), kv_width:] = v_ref[pl.ds(src, SPAN), :]
        acc_ref[pl.ds(src, SPAN), :] = jnp.zeros((SPAN, 2 * kv_width), jnp.float32)
        return 0

    lax.fori_loop(0, num_spans, to_sequence, 0)

    def rows_of(ref, span, head):
        return jnp.concatenate(
            [
                ref[
                    span * SPAN : (span + 1) * SPAN,
                    (head * GROUP + j) * HD : (head * GROUP + j + 1) * HD,
                ]
                for j in range(GROUP)
            ],
            axis=0,
        )

    def write_rows(ref, span, head, block):
        for j in range(GROUP):
            ref[
                span * SPAN : (span + 1) * SPAN,
                (head * GROUP + j) * HD : (head * GROUP + j + 1) * HD,
            ] = block[j * SPAN : (j + 1) * SPAN, :]

    def key_cols(head):
        return slice(head * HD, (head + 1) * HD)

    def value_cols(head):
        return slice(kv_width + head * HD, kv_width + (head + 1) * HD)

    def first_with(doc, low, high, rounds):
        def halve(_, ends):
            low, high = ends
            mid = (low + high) // 2
            below = docs_ref[mid] < doc
            return jnp.where(below, mid + 1, low), jnp.where(below, high, mid)

        return lax.fori_loop(0, rounds, halve, (low, high))[1]

    for span in range(CPR):
        begin = spans_ref[rank_ref[0] * CPR + span] * SPAN
        doc_low = docs_ref[begin]
        doc_high = docs_ref[begin + SPAN - 1]
        pos = begin + lax.broadcasted_iota(jnp.int32, (1, ROWS), 1) % SPAN
        lowest = first_with(doc_low, 0, begin, 11)
        first = lowest // CHUNK
        last = begin // CHUNK + 1

        def next_doc(doc, start):
            bound = first_with(doc, begin, begin + SPAN - 1, 6)
            return jnp.where(pos >= bound, bound, start)

        start = lax.fori_loop(
            doc_low + 1, doc_high + 1, next_doc, jnp.full((1, ROWS), lowest, jnp.int32)
        )

        def score_step(c, carry):
            rows = pl.ds(pl.multiple_of(c * CHUNK, CHUNK), CHUNK)
            key_pos = lax.broadcasted_iota(jnp.int32, (CHUNK, ROWS), 0) + c * CHUNK
            keep = (key_pos >= start) & (key_pos <= pos)
            out = []
            for head in range(KVH):
                top, total = carry[head]
                s = mm(seq_ref[rows, key_cols(head)], rows_of(q_ref, span, head), NT)
                s = jnp.where(keep, s * LOG2_SCALE, FAR)
                s_ref[head, c] = s
                new_top = jnp.maximum(top, jnp.max(s, axis=0, keepdims=True))
                new_total = total * jnp.exp2(top - new_top) + jnp.sum(
                    jnp.exp2(s - new_top), axis=0, keepdims=True
                )
                out.append((new_top, new_total))
            return tuple(out)

        empty = (jnp.full((1, ROWS), FAR, jnp.float32), jnp.zeros((1, ROWS), jnp.float32))
        stats = lax.fori_loop(first, last, score_step, (empty,) * KVH)
        log_total = [top + jnp.log2(total) for top, total in stats]
        t_ref[...] = jnp.zeros_like(t_ref)

        def value_step(c, _):
            rows = pl.ds(pl.multiple_of(c * CHUNK, CHUNK), CHUNK)
            for head in range(KVH):
                p = jnp.exp2(s_ref[head, c] - log_total[head]).astype(jnp.bfloat16)
                p_ref[head, c] = p
                t_ref[head] += mm(seq_ref[rows, value_cols(head)], p, TN)
                acc_ref[rows, value_cols(head)] += mm(p, rows_of(do_ref, span, head), NN)
            return 0

        lax.fori_loop(first, last, value_step, 0)
        delta = []
        for head in range(KVH):
            out_t = t_ref[head].astype(jnp.bfloat16).astype(jnp.float32)
            grad_t = rows_of(do_ref, span, head).astype(jnp.float32).T
            delta.append(jnp.sum(out_t * grad_t, axis=0, keepdims=True))
            write_rows(o_ref, span, head, out_t.T.astype(jnp.bfloat16))
        t_ref[...] = jnp.zeros_like(t_ref)

        def grad_step(c, _):
            rows = pl.ds(pl.multiple_of(c * CHUNK, CHUNK), CHUNK)
            for head in range(KVH):
                dp = mm(seq_ref[rows, value_cols(head)], rows_of(do_ref, span, head), NT)
                ds = (p_ref[head, c].astype(jnp.float32) * (dp - delta[head])).astype(jnp.bfloat16)
                t_ref[head] += mm(seq_ref[rows, key_cols(head)], ds, TN)
                acc_ref[rows, key_cols(head)] += mm(ds, rows_of(q_ref, span, head), NN)
            return 0

        lax.fori_loop(first, last, grad_step, 0)
        for head in range(KVH):
            write_rows(dq_ref, span, head, (t_ref[head] * INV_ROOT).T.astype(jnp.bfloat16))

    def to_layout(i, _):
        dst = pl.multiple_of(i * SPAN, SPAN)
        src = pl.multiple_of(spans_ref[i] * SPAN, SPAN)
        dkv_ref[pl.ds(dst, SPAN), 0:kv_width] = (
            acc_ref[pl.ds(src, SPAN), 0:kv_width] * INV_ROOT
        ).astype(jnp.bfloat16)
        dkv_ref[pl.ds(dst, SPAN), kv_width:] = acc_ref[pl.ds(src, SPAN), kv_width:].astype(
            jnp.bfloat16
        )
        return 0

    lax.fori_loop(0, num_spans, to_layout, 0)


def attention(queries, cotangent, k_all, v_all, doc_list, span_list, rank_index):
    tokens, width = queries.shape
    seq_len = k_all.shape[0]
    kv_width = 2 * k_all.shape[1]
    chunks = seq_len // CHUNK
    vmem = pl.BlockSpec(memory_space=pltpu.VMEM)
    smem = pl.BlockSpec(memory_space=pltpu.SMEM)
    return pl.pallas_call(
        attention_kernel,
        out_shape=(
            jax.ShapeDtypeStruct((tokens, width), jnp.bfloat16),
            jax.ShapeDtypeStruct((tokens, width), jnp.bfloat16),
            jax.ShapeDtypeStruct((seq_len, kv_width), jnp.bfloat16),
        ),
        in_specs=[smem, smem, smem, vmem, vmem, vmem, vmem],
        out_specs=(vmem, vmem, vmem),
        scratch_shapes=[
            pltpu.VMEM((seq_len, kv_width), jnp.bfloat16),
            pltpu.VMEM((seq_len, kv_width), jnp.float32),
            pltpu.VMEM((KVH, chunks, CHUNK, ROWS), jnp.float32),
            pltpu.VMEM((KVH, chunks, CHUNK, ROWS), jnp.bfloat16),
            pltpu.VMEM((KVH, HD, ROWS), jnp.float32),
        ],
        compiler_params=pltpu.CompilerParams(vmem_limit_bytes=40 * 1024 * 1024),
        cost_estimate=pl.CostEstimate(
            flops=12 * tokens * HQ * HD * seq_len // 2,
            bytes_accessed=8 * tokens * width + 4 * seq_len * kv_width,
            transcendentals=tokens * HQ * seq_len,
        ),
        name="attention",
    )(
        span_list,
        jnp.reshape(rank_index, (1,)),
        doc_list,
        queries,
        cotangent,
        k_all,
        v_all,
    )


def ring_place():
    me = lax.axis_index("ctx")
    y, core = me // 2, me % 2

    def at(chip, which):
        return {"ctx": lax.rem(chip + RING, RING) * 2 + which}

    return y, core, at(y + 1, core), at(y - 1, core), at(y, 1 - core)


def greet(partners):
    barrier = pltpu.get_barrier_semaphore()
    for partner in partners:
        pl.semaphore_signal(barrier, inc=1, device_id=partner, device_id_type=MESH)
    pl.semaphore_wait(barrier, len(partners))


def push(src, dst, send_sem, recv_sem, target):
    return pltpu.make_async_remote_copy(
        src_ref=src,
        dst_ref=dst,
        send_sem=send_sem,
        recv_sem=recv_sem,
        device_id=target,
        device_id_type=MESH,
    )


def carried(direction, step, half, short_step):
    return step != short_step or half == direction


class RingGather:
    def __init__(self, a, own_ref, all_ref, sems, place):
        self.a, self.own_ref, self.all_ref = a, own_ref, all_ref
        self.rows = own_ref.shape[0]
        (
            self.local_sem,
            self.ring_send,
            self.ring_recv,
            self.own_send,
            self.own_recv,
            self.sib_send,
            self.sib_recv,
        ) = sems
        self.y, self.core, self.right, self.left, self.sibling = place
        self.sent = []

    def piece(self, chip, which, half):
        rows = self.rows // 2
        start = (lax.rem(chip + RING, RING) * 4 + which * 2 + half) * rows
        return self.all_ref.at[pl.ds(pl.multiple_of(start, rows), rows), :]

    def block(self, chip, which):
        start = (lax.rem(chip + RING, RING) * 2 + which) * self.rows
        return self.all_ref.at[pl.ds(pl.multiple_of(start, self.rows), self.rows), :]

    def send(self, copy):
        copy.start()
        self.sent.append(copy)

    def along(self, src, dst, direction, step, half):
        return push(
            src,
            dst,
            self.ring_send.at[self.a, direction, step, half],
            self.ring_recv.at[self.a, direction, step, half],
            self.left if direction else self.right,
        )

    def across(self, ref, direction, step, half):
        return push(
            ref,
            ref,
            self.sib_send.at[self.a, direction, step, half],
            self.sib_recv.at[self.a, direction, step, half],
            self.sibling,
        )

    def own_across(self, src, dst):
        return push(src, dst, self.own_send.at[self.a], self.own_recv.at[self.a], self.sibling)

    def start(self):
        rows = self.rows // 2
        for half in range(2):
            for direction in range(2):
                src = self.own_ref.at[pl.ds(half * rows, rows), :]
                dst = self.piece(self.y, self.core, half)
                self.send(self.along(src, dst, direction, 0, half))
        mine = self.block(self.y, self.core)
        self.send(self.own_across(self.own_ref, mine))
        self.local = pltpu.make_async_copy(self.own_ref, mine, self.local_sem.at[self.a])
        self.local.start()

    def pieces(self, step):
        for half in range(2):
            for direction in range(2):
                if carried(direction, step, half, STEPS - 1):
                    chip = self.y + 1 + step if direction else self.y - 1 - step
                    yield direction, half, chip

    def step(self, step):
        for direction, half, chip in self.pieces(step):
            here = self.piece(chip, self.core, half)
            self.along(here, here, direction, step, half).wait_recv()
            if step + 1 < STEPS and carried(direction, step + 1, half, STEPS - 1):
                self.send(self.along(here, here, direction, step + 1, half))
            self.send(self.across(here, direction, step, half))

    def own_from_sibling(self):
        there = self.block(self.y, 1 - self.core)
        self.own_across(there, there).wait_recv()

    def from_sibling(self, step):
        for direction, half, chip in self.pieces(step):
            there = self.piece(chip, 1 - self.core, half)
            self.across(there, direction, step, half).wait_recv()

    def finish(self):
        self.local.wait()
        for copy in self.sent:
            copy.wait_send()


def front_kernel(
    hidden_ref,
    weight_ref,
    keys_ref,
    weight_out,
    key_out,
    value_out,
    weight_all,
    acc_ref,
    values_ref,
    out_sem,
    *sems,
):
    place = ring_place()
    y, core = place[:2]
    greet(place[2:])
    weight = RingGather(0, weight_ref, weight_all, sems, place)
    key = RingGather(1, keys_ref, key_out, sems, place)
    value = RingGather(2, values_ref, value_out, sems, place)
    depth = weight_ref.shape[0]

    def project(chip, which):
        start = (lax.rem(chip + RING, RING) * 2 + which) * depth
        rows = pl.ds(pl.multiple_of(start, depth), depth)
        acc_ref[...] += mm(hidden_ref[:, rows], weight_all[rows, :], NN)

    weight.start()
    acc_ref[...] = jnp.zeros_like(acc_ref)
    for step in range(STEPS):
        weight.step(step)
        if step == STEPS - 2:
            key.start()
        if step == 0:
            weight.local.wait()
            project(y, core)
            weight.own_from_sibling()
            project(y, 1 - core)
        else:
            weight.from_sibling(step - 1)
            project(y - step, 1 - core)
            project(y + step, 1 - core)
        project(y - 1 - step, core)
        if step < STEPS - 1:
            project(y + 1 + step, core)
    weight.from_sibling(STEPS - 1)
    project(y + STEPS, 1 - core)
    values_ref[...] = acc_ref[...].astype(jnp.bfloat16)
    value.start()
    keep = pltpu.make_async_copy(weight_all, weight_out, out_sem)
    keep.start()
    for step in range(STEPS):
        key.step(step)
        value.step(step)
    for each in (key, value):
        each.own_from_sibling()
        for step in range(STEPS):
            each.from_sibling(step)
    keep.wait()
    for each in (key, value):
        each.finish()
    for copy in weight.sent:
        copy.wait_send()


def front(hidden, value_weight, keys, collective_id):
    tokens, kv_width = keys.shape
    ring = pltpu.SemaphoreType.DMA((3, 2, STEPS, 2))
    one = pltpu.SemaphoreType.DMA((3,))
    anywhere = pl.BlockSpec(memory_space=pl.ANY)
    vmem = pl.BlockSpec(memory_space=pltpu.VMEM)
    depth = value_weight.shape[0] * 2 * RING
    gathered = jax.ShapeDtypeStruct((tokens * 2 * RING, kv_width), keys.dtype)
    return pl.pallas_call(
        front_kernel,
        out_shape=(
            jax.ShapeDtypeStruct((depth, kv_width), value_weight.dtype),
            gathered,
            gathered,
        ),
        in_specs=[vmem, vmem, vmem],
        out_specs=(anywhere,) * 3,
        scratch_shapes=[
            pltpu.VMEM((depth, kv_width), jnp.bfloat16),
            pltpu.VMEM((tokens, kv_width), jnp.float32),
            pltpu.VMEM((tokens, kv_width), jnp.bfloat16),
            pltpu.SemaphoreType.DMA,
            one,
            ring,
            ring,
            one,
            one,
            ring,
            ring,
        ],
        compiler_params=pltpu.CompilerParams(
            collective_id=collective_id,
            has_side_effects=True,
            vmem_limit_bytes=24 * 1024 * 1024,
        ),
        cost_estimate=pl.CostEstimate(
            flops=2 * tokens * depth * kv_width,
            bytes_accessed=4 * depth * kv_width,
            transcendentals=0,
        ),
        name="front",
    )(hidden, value_weight, keys)


NEAR = (4, 3, -3, 2, -2, 1, -1, 0)


class RingReduce:
    def __init__(self, term, send_ref, recv_ref, ring_send, ring_recv, place):
        self.term, self.send_ref, self.recv_ref = term, send_ref, recv_ref
        self.ring_send, self.ring_recv = ring_send, ring_recv
        self.targets = place[2:4]
        self.sent = []

    def copy(self, src, direction, step, half):
        return push(
            src,
            self.recv_ref.at[direction, step, half],
            self.ring_send.at[direction, step, half],
            self.ring_recv.at[direction, step, half],
            self.targets[direction],
        )

    def arrived(self, direction, step, half):
        self.copy(self.send_ref.at[direction, step, half], direction, step, half).wait_recv()
        return self.recv_ref[direction, step, half].astype(jnp.float32)

    def step(self, step):
        distance = STEPS - step
        for half in range(2):
            for direction in range(2):
                if not carried(direction, step, half, 0):
                    continue
                value = self.term(-distance if direction else distance, half)
                if step > 0 and carried(direction, step - 1, half, 0):
                    value = value + self.arrived(direction, step - 1, half)
                self.send_ref[direction, step, half] = value.astype(jnp.bfloat16)
                copy = self.copy(self.send_ref.at[direction, step, half], direction, step, half)
                copy.start()
                self.sent.append(copy)

    def result(self, half):
        value = self.term(0, half)
        for direction in range(2):
            value = value + self.arrived(direction, STEPS - 1, half)
        return value


class FromSibling:
    def __init__(self, land_ref, send_sem, recv_sem, sibling):
        self.land_ref, self.send_sem, self.recv_sem = land_ref, send_sem, recv_sem
        self.sibling = sibling
        self.sent = []
        self.waited = set()

    def copy(self, i, src):
        return push(
            src, self.land_ref.at[i], self.send_sem.at[i], self.recv_sem.at[i], self.sibling
        )

    def send(self, i, src):
        copy = self.copy(i, src)
        copy.start()
        self.sent.append(copy)

    def half_block(self, offset, half):
        i = NEAR.index(4 if offset == -4 else offset)
        if i not in self.waited:
            self.waited.add(i)
            self.copy(i, self.land_ref.at[i]).wait_recv()
        rows = self.land_ref.shape[1] // 2
        return self.land_ref[i, half * rows : (half + 1) * rows, :].astype(jnp.float32)


def back_kernel(
    terms_ref,
    hidden_ref,
    key_out,
    value_out,
    weight_out,
    t_land,
    t_send,
    t_recv,
    w_stage,
    w_land,
    w_send,
    w_recv,
    grads_ref,
    own_ref,
    z_land,
    part_ref,
    x_slots,
    total_ref,
    t_sib_send,
    t_sib_recv,
    t_ring_send,
    t_ring_recv,
    w_sib_send,
    w_sib_recv,
    w_ring_send,
    w_ring_recv,
    z_send,
    z_recv,
    x_send,
    x_recv,
    g_send,
    g_recv,
):
    place = ring_place()
    y, core = place[:2]
    sibling = place[4]
    dp = lax.axis_index("dp")
    z, x = dp // N_X, dp % N_X
    z_after = [{"dp": lax.rem(z + k, N_Z) * N_X + x} for k in range(1, N_Z)]
    x_after = [{"dp": z * N_X + lax.rem(x + k, N_X)} for k in range(1, N_X)]
    greet(tuple(place[2:]) + tuple(z_after) + tuple(x_after))

    tokens = hidden_ref.shape[0]
    width = key_out.shape[1]
    depth = own_ref.shape[0]

    def owner(offset, which):
        return lax.rem(y + offset + RING, RING) * 2 + which

    def term_sums(n, first_col):
        cols = slice(first_col, first_col + width)
        sib = FromSibling(t_land.at[n], t_sib_send.at[n], t_sib_recv.at[n], sibling)
        for i, offset in enumerate(NEAR):
            start = pl.multiple_of(owner(offset, 1 - core) * tokens, tokens)
            sib.send(i, terms_ref.at[pl.ds(start, tokens), cols])

        def term(offset, half):
            rows = tokens // 2
            start = pl.multiple_of(owner(offset, core) * tokens + half * rows, rows)
            mine = terms_ref[pl.ds(start, rows), cols].astype(jnp.float32)
            return mine + sib.half_block(offset, half)

        ring = RingReduce(
            term, t_send.at[n], t_recv.at[n], t_ring_send.at[n], t_ring_recv.at[n], place
        )
        return ring, sib

    value, value_sib = term_sums(0, width)
    key, key_sib = term_sums(1, 0)
    value.step(0)
    value.step(1)
    key.step(0)
    value.step(2)
    key.step(1)
    value.step(3)
    key.step(2)
    rows = tokens // 2
    for half in range(2):
        grads_ref[half * rows : (half + 1) * rows, :] = value.result(half).astype(jnp.bfloat16)

    def partial(offset, which, first_row, count):
        start = pl.multiple_of(owner(offset, which) * depth + first_row, count)
        return mm(hidden_ref[:, pl.ds(start, count)], grads_ref[...], TN)

    weight_sib = FromSibling(w_land, w_sib_send, w_sib_recv, sibling)

    def weight_term(offset, half):
        mine = partial(offset, core, half * (depth // 2), depth // 2)
        return mine + weight_sib.half_block(offset, half)

    weight = RingReduce(weight_term, w_send, w_recv, w_ring_send, w_ring_recv, place)

    def stage(*order):
        for i in order:
            w_stage[i] = partial(NEAR[i], 1 - core, 0, depth).astype(jnp.bfloat16)
            weight_sib.send(i, w_stage.at[i])

    stage(0, 1, 2)
    weight.step(0)
    key.step(3)
    stage(3, 4)
    weight.step(1)
    stage(5, 6, 7)
    weight.step(2)
    value_out[...] = grads_ref[...]
    for half in range(2):
        key_out[half * rows : (half + 1) * rows, :] = key.result(half).astype(jnp.bfloat16)
    weight.step(3)

    sent = value.sent + key.sent + weight.sent
    sent += value_sib.sent + key_sib.sent + weight_sib.sent
    half_depth = depth // 2
    part = half_depth // N_Z

    def z_rows(half, who):
        start = half * half_depth + lax.rem(who + N_Z, N_Z) * part
        return pl.ds(pl.multiple_of(start, part), part)

    def z_copy(half, k):
        return push(
            own_ref.at[z_rows(half, z + k), :],
            z_land.at[half, k - 1],
            z_send.at[half, k - 1],
            z_recv.at[half, k - 1],
            z_after[k - 1],
        )

    def x_copy(half, k, who):
        return push(
            part_ref.at[half],
            x_slots.at[half, lax.rem(who + N_X, N_X)],
            x_send.at[half, k - 1],
            x_recv.at[half, k - 1],
            x_after[k - 1],
        )

    def g_copy(half, k, who):
        there = total_ref.at[z_rows(half, who), :]
        return push(
            there, there, g_send.at[half, k - 1], g_recv.at[half, k - 1], z_after[k - 1]
        )

    for half in range(2):
        own_ref[half * half_depth : (half + 1) * half_depth, :] = weight.result(half).astype(
            jnp.bfloat16
        )
        for k in range(1, N_Z):
            copy = z_copy(half, k)
            copy.start()
            sent.append(copy)
    for half in range(2):
        total = own_ref[z_rows(half, z), :].astype(jnp.float32)
        for k in range(1, N_Z):
            z_copy(half, k).wait_recv()
            total = total + z_land[half, k - 1].astype(jnp.float32)
        part_ref[half] = total.astype(jnp.bfloat16)
        x_slots[half, x] = part_ref[half]
        for k in range(1, N_X):
            copy = x_copy(half, k, x)
            copy.start()
            sent.append(copy)
    for half in range(2):
        for k in range(1, N_X):
            x_copy(half, k, x - k).wait_recv()
        total = x_slots[half, 0].astype(jnp.float32)
        for k in range(1, N_X):
            total = total + x_slots[half, k].astype(jnp.float32)
        total_ref[z_rows(half, z), :] = (total * (1.0 / (N_Z * N_X))).astype(jnp.bfloat16)
        for k in range(1, N_Z):
            copy = g_copy(half, k, z)
            copy.start()
            sent.append(copy)
    for half in range(2):
        for k in range(1, N_Z):
            g_copy(half, k, z - k).wait_recv()
    weight_out[...] = total_ref[...]
    for copy in sent:
        copy.wait_send()


def back(terms, hidden, collective_id):
    tokens, features = hidden.shape
    width = terms.shape[1] // 2
    depth = features // (2 * RING)
    part = depth // 2 // N_Z
    vmem = pl.BlockSpec(memory_space=pltpu.VMEM)

    def buffer(*shape):
        return pltpu.VMEM(shape, jnp.bfloat16)

    def dma(*shape):
        return pltpu.SemaphoreType.DMA(shape)

    t_slots = buffer(2, 2, STEPS, 2, tokens // 2, width)
    w_slots = buffer(2, STEPS, 2, depth // 2, width)
    return pl.pallas_call(
        back_kernel,
        out_shape=(
            jax.ShapeDtypeStruct((tokens, width), jnp.bfloat16),
            jax.ShapeDtypeStruct((tokens, width), jnp.bfloat16),
            jax.ShapeDtypeStruct((depth, width), jnp.bfloat16),
        ),
        in_specs=[vmem, vmem],
        out_specs=(vmem,) * 3,
        scratch_shapes=[
            buffer(2, RING, tokens, width),
            t_slots,
            t_slots,
            buffer(RING, depth, width),
            buffer(RING, depth, width),
            w_slots,
            w_slots,
            buffer(tokens, width),
            buffer(depth, width),
            buffer(2, N_Z - 1, part, width),
            buffer(2, part, width),
            buffer(2, N_X, part, width),
            buffer(depth, width),
            dma(2, RING),
            dma(2, RING),
            dma(2, 2, STEPS, 2),
            dma(2, 2, STEPS, 2),
            dma(RING),
            dma(RING),
            dma(2, STEPS, 2),
            dma(2, STEPS, 2),
            dma(2, N_Z - 1),
            dma(2, N_Z - 1),
            dma(2, N_X - 1),
            dma(2, N_X - 1),
            dma(2, N_Z - 1),
            dma(2, N_Z - 1),
        ],
        compiler_params=pltpu.CompilerParams(
            collective_id=collective_id,
            has_side_effects=True,
            vmem_limit_bytes=36 * 1024 * 1024,
        ),
        cost_estimate=pl.CostEstimate(
            flops=2 * hidden.size * width, bytes_accessed=4 * terms.size, transcendentals=0
        ),
        name="back",
    )(terms, hidden)


def per_device(hidden, queries, keys, cotangent, value_weight, doc_ids, span_order):
    rank_index = lax.axis_index("ctx")
    token_rows = hidden[0]
    weight_all, key_all, value_all = front(token_rows, value_weight, keys[0], 0)
    attention_out, query_grads, kv_terms = attention(
        queries[0], cotangent[0], key_all, value_all, doc_ids[0], span_order[0], rank_index
    )
    key_own, value_own, weight_grads = back(kv_terms, token_rows, 1)
    input_grads = lax.dot_general(
        value_own, weight_all, NT, preferred_element_type=jnp.float32
    ).astype(jnp.bfloat16)
    return (
        attention_out[None],
        query_grads[None],
        key_own[None],
        input_grads[None],
        weight_grads,
    )


def solution(mesh):
    return jax.shard_map(
        per_device,
        mesh=mesh,
        in_specs=(
            P("dp", "ctx", None),
            P("dp", "ctx", None),
            P("dp", "ctx", None),
            P("dp", "ctx", None),
            P("ctx", None),
            P("dp", None),
            P("dp", None),
        ),
        out_specs=(
            P("dp", "ctx", None),
            P("dp", "ctx", None),
            P("dp", "ctx", None),
            P("dp", "ctx", None),
            P("ctx", None),
        ),
        check_vma=False,
    )
```

```python
import functools
import math

import jax
import jax.numpy as jnp
from jax import lax
from jax.experimental import pallas as pl
from jax.experimental.pallas import tpu as pltpu
from jax.sharding import PartitionSpec as P

HQ = 16
KVH = 4
HD = 128
CPR = 2
SPAN = 64
CHUNK = 256
GROUP = HQ // KVH
ROWS = SPAN * GROUP
INV_ROOT = 1.0 / math.sqrt(HD)
LOG2_SCALE = INV_ROOT * math.log2(math.e)
FAR = -1e30
RING = 8
N_Z = 8
N_X = 4
STEPS = RING // 2
MESH = pl.DeviceIdType.MESH

NT = (((1,), (1,)), ((), ()))
TN = (((0,), (0,)), ((), ()))
NN = (((1,), (0,)), ((), ()))


def mm(a, b, dims):
    return lax.dot_general(a, b, dims, preferred_element_type=jnp.float32)


def attention_kernel(
    spans_ref,
    rank_ref,
    docs_ref,
    q_ref,
    do_ref,
    k_ref,
    v_ref,
    o_ref,
    dq_ref,
    dkv_ref,
    seq_ref,
    acc_ref,
    s_ref,
    p_ref,
    t_ref,
):
    num_spans = spans_ref.shape[0]
    kv_width = KVH * HD

    def to_sequence(i, _):
        src = pl.multiple_of(i * SPAN, SPAN)
        dst = pl.multiple_of(spans_ref[i] * SPAN, SPAN)
        seq_ref[pl.ds(dst, SPAN), 0:kv_width] = k_ref[pl.ds(src, SPAN), :]
        seq_ref[pl.ds(dst, SPAN), kv_width:] = v_ref[pl.ds(src, SPAN), :]
        acc_ref[pl.ds(src, SPAN), :] = jnp.zeros((SPAN, 2 * kv_width), jnp.float32)
        return 0

    lax.fori_loop(0, num_spans, to_sequence, 0)

    def rows_of(ref, span, head):
        return jnp.concatenate(
            [
                ref[
                    span * SPAN : (span + 1) * SPAN,
                    (head * GROUP + j) * HD : (head * GROUP + j + 1) * HD,
                ]
                for j in range(GROUP)
            ],
            axis=0,
        )

    def write_rows(ref, span, head, block):
        for j in range(GROUP):
            ref[
                span * SPAN : (span + 1) * SPAN,
                (head * GROUP + j) * HD : (head * GROUP + j + 1) * HD,
            ] = block[j * SPAN : (j + 1) * SPAN, :]

    def key_cols(head):
        return slice(head * HD, (head + 1) * HD)

    def value_cols(head):
        return slice(kv_width + head * HD, kv_width + (head + 1) * HD)

    def first_with(doc, low, high, rounds):
        def halve(_, ends):
            low, high = ends
            mid = (low + high) // 2
            below = docs_ref[mid] < doc
            return jnp.where(below, mid + 1, low), jnp.where(below, high, mid)

        return lax.fori_loop(0, rounds, halve, (low, high))[1]

    for span in range(CPR):
        begin = spans_ref[rank_ref[0] * CPR + span] * SPAN
        doc_low = docs_ref[begin]
        doc_high = docs_ref[begin + SPAN - 1]
        pos = begin + lax.broadcasted_iota(jnp.int32, (1, ROWS), 1) % SPAN
        lowest = first_with(doc_low, 0, begin, 11)
        first = lowest // CHUNK
        last = begin // CHUNK + 1

        def next_doc(doc, start):
            bound = first_with(doc, begin, begin + SPAN - 1, 6)
            return jnp.where(pos >= bound, bound, start)

        start = lax.fori_loop(
            doc_low + 1, doc_high + 1, next_doc, jnp.full((1, ROWS), lowest, jnp.int32)
        )

        def score_step(c, carry):
            rows = pl.ds(pl.multiple_of(c * CHUNK, CHUNK), CHUNK)
            key_pos = lax.broadcasted_iota(jnp.int32, (CHUNK, ROWS), 0) + c * CHUNK
            keep = (key_pos >= start) & (key_pos <= pos)
            out = []
            for head in range(KVH):
                top, total = carry[head]
                s = mm(seq_ref[rows, key_cols(head)], rows_of(q_ref, span, head), NT)
                s = jnp.where(keep, s * LOG2_SCALE, FAR)
                s_ref[head, c] = s
                new_top = jnp.maximum(top, jnp.max(s, axis=0, keepdims=True))
                new_total = total * jnp.exp2(top - new_top) + jnp.sum(
                    jnp.exp2(s - new_top), axis=0, keepdims=True
                )
                out.append((new_top, new_total))
            return tuple(out)

        empty = (jnp.full((1, ROWS), FAR, jnp.float32), jnp.zeros((1, ROWS), jnp.float32))
        stats = lax.fori_loop(first, last, score_step, (empty,) * KVH)
        log_total = [top + jnp.log2(total) for top, total in stats]
        t_ref[...] = jnp.zeros_like(t_ref)

        def value_step(c, _):
            rows = pl.ds(pl.multiple_of(c * CHUNK, CHUNK), CHUNK)
            for head in range(KVH):
                p = jnp.exp2(s_ref[head, c] - log_total[head]).astype(jnp.bfloat16)
                p_ref[head, c] = p
                t_ref[head] += mm(seq_ref[rows, value_cols(head)], p, TN)
                acc_ref[rows, value_cols(head)] += mm(p, rows_of(do_ref, span, head), NN)
            return 0

        lax.fori_loop(first, last, value_step, 0)
        delta = []
        for head in range(KVH):
            out_t = t_ref[head].astype(jnp.bfloat16).astype(jnp.float32)
            grad_t = rows_of(do_ref, span, head).astype(jnp.float32).T
            delta.append(jnp.sum(out_t * grad_t, axis=0, keepdims=True))
            write_rows(o_ref, span, head, out_t.T.astype(jnp.bfloat16))
        t_ref[...] = jnp.zeros_like(t_ref)

        def grad_step(c, _):
            rows = pl.ds(pl.multiple_of(c * CHUNK, CHUNK), CHUNK)
            for head in range(KVH):
                dp = mm(seq_ref[rows, value_cols(head)], rows_of(do_ref, span, head), NT)
                ds = (p_ref[head, c].astype(jnp.float32) * (dp - delta[head])).astype(jnp.bfloat16)
                t_ref[head] += mm(seq_ref[rows, key_cols(head)], ds, TN)
                acc_ref[rows, key_cols(head)] += mm(ds, rows_of(q_ref, span, head), NN)
            return 0

        lax.fori_loop(first, last, grad_step, 0)
        for head in range(KVH):
            write_rows(dq_ref, span, head, (t_ref[head] * INV_ROOT).T.astype(jnp.bfloat16))

    def to_layout(i, _):
        dst = pl.multiple_of(i * SPAN, SPAN)
        src = pl.multiple_of(spans_ref[i] * SPAN, SPAN)
        dkv_ref[pl.ds(dst, SPAN), 0:kv_width] = (
            acc_ref[pl.ds(src, SPAN), 0:kv_width] * INV_ROOT
        ).astype(jnp.bfloat16)
        dkv_ref[pl.ds(dst, SPAN), kv_width:] = acc_ref[pl.ds(src, SPAN), kv_width:].astype(
            jnp.bfloat16
        )
        return 0

    lax.fori_loop(0, num_spans, to_layout, 0)


def attention(queries, cotangent, k_all, v_all, doc_list, span_list, rank_index):
    tokens, width = queries.shape
    seq_len = k_all.shape[0]
    kv_width = 2 * k_all.shape[1]
    chunks = seq_len // CHUNK
    vmem = pl.BlockSpec(memory_space=pltpu.VMEM)
    smem = pl.BlockSpec(memory_space=pltpu.SMEM)
    return pl.pallas_call(
        attention_kernel,
        out_shape=(
            jax.ShapeDtypeStruct((tokens, width), jnp.bfloat16),
            jax.ShapeDtypeStruct((tokens, width), jnp.bfloat16),
            jax.ShapeDtypeStruct((seq_len, kv_width), jnp.bfloat16),
        ),
        in_specs=[smem, smem, smem, vmem, vmem, vmem, vmem],
        out_specs=(vmem, vmem, vmem),
        scratch_shapes=[
            pltpu.VMEM((seq_len, kv_width), jnp.bfloat16),
            pltpu.VMEM((seq_len, kv_width), jnp.float32),
            pltpu.VMEM((KVH, chunks, CHUNK, ROWS), jnp.float32),
            pltpu.VMEM((KVH, chunks, CHUNK, ROWS), jnp.bfloat16),
            pltpu.VMEM((KVH, HD, ROWS), jnp.float32),
        ],
        compiler_params=pltpu.CompilerParams(vmem_limit_bytes=40 * 1024 * 1024),
        cost_estimate=pl.CostEstimate(
            flops=12 * tokens * HQ * HD * seq_len // 2,
            bytes_accessed=8 * tokens * width + 4 * seq_len * kv_width,
            transcendentals=tokens * HQ * seq_len,
        ),
        name="attention",
    )(
        span_list,
        jnp.reshape(rank_index, (1,)),
        doc_list,
        queries,
        cotangent,
        k_all,
        v_all,
    )


def ring_place():
    me = lax.axis_index("ctx")
    y, core = me // 2, me % 2

    def at(chip, which):
        return {"ctx": lax.rem(chip + RING, RING) * 2 + which}

    return y, core, at(y + 1, core), at(y - 1, core), at(y, 1 - core)


def greet(partners):
    barrier = pltpu.get_barrier_semaphore()
    for partner in partners:
        pl.semaphore_signal(barrier, inc=1, device_id=partner, device_id_type=MESH)
    pl.semaphore_wait(barrier, len(partners))


def push(src, dst, send_sem, recv_sem, target):
    return pltpu.make_async_remote_copy(
        src_ref=src,
        dst_ref=dst,
        send_sem=send_sem,
        recv_sem=recv_sem,
        device_id=target,
        device_id_type=MESH,
    )


def carried(direction, step, half, short_step):
    return step != short_step or half == direction


class RingGather:
    def __init__(self, a, own_ref, all_ref, sems, place, stride=None):
        self.a, self.own_ref, self.all_ref = a, own_ref, all_ref
        self.rows = own_ref.shape[0]
        self.stride = stride or self.rows
        (
            self.local_sem,
            self.ring_send,
            self.ring_recv,
            self.own_send,
            self.own_recv,
            self.sib_send,
            self.sib_recv,
        ) = sems
        self.y, self.core, self.right, self.left, self.sibling = place
        self.sent = []

    def piece(self, chip, which, half):
        rows = self.rows // 2
        start = (lax.rem(chip + RING, RING) * 2 + which) * self.stride + half * rows
        return self.all_ref.at[pl.ds(pl.multiple_of(start, rows), rows), :]

    def block(self, chip, which):
        start = (lax.rem(chip + RING, RING) * 2 + which) * self.stride
        return self.all_ref.at[pl.ds(pl.multiple_of(start, self.rows), self.rows), :]

    def send(self, copy):
        copy.start()
        self.sent.append(copy)

    def along(self, src, dst, direction, step, half):
        return push(
            src,
            dst,
            self.ring_send.at[self.a, direction, step, half],
            self.ring_recv.at[self.a, direction, step, half],
            self.left if direction else self.right,
        )

    def across(self, ref, direction, step, half):
        return push(
            ref,
            ref,
            self.sib_send.at[self.a, direction, step, half],
            self.sib_recv.at[self.a, direction, step, half],
            self.sibling,
        )

    def own_across(self, src, dst):
        return push(src, dst, self.own_send.at[self.a], self.own_recv.at[self.a], self.sibling)

    def start(self, in_place=False):
        rows = self.rows // 2
        for half in range(2):
            for direction in range(2):
                src = self.own_ref.at[pl.ds(half * rows, rows), :]
                dst = self.piece(self.y, self.core, half)
                self.send(self.along(src, dst, direction, 0, half))
        mine = self.block(self.y, self.core)
        self.send(self.own_across(self.own_ref, mine))
        if not in_place:
            self.local = pltpu.make_async_copy(self.own_ref, mine, self.local_sem.at[self.a])
            self.local.start()

    def pieces(self, step):
        for half in range(2):
            for direction in range(2):
                if carried(direction, step, half, STEPS - 1):
                    chip = self.y + 1 + step if direction else self.y - 1 - step
                    yield direction, half, chip

    def step(self, step):
        for direction, half, chip in self.pieces(step):
            here = self.piece(chip, self.core, half)
            self.along(here, here, direction, step, half).wait_recv()
            if step + 1 < STEPS and carried(direction, step + 1, half, STEPS - 1):
                self.send(self.along(here, here, direction, step + 1, half))
            self.send(self.across(here, direction, step, half))

    def own_from_sibling(self):
        there = self.block(self.y, 1 - self.core)
        self.own_across(there, there).wait_recv()

    def from_sibling(self, step):
        for direction, half, chip in self.pieces(step):
            there = self.piece(chip, 1 - self.core, half)
            self.across(there, direction, step, half).wait_recv()

    def finish(self):
        self.local.wait()
        for copy in self.sent:
            copy.wait_send()


def front_kernel(
    hidden_ref,
    weight_ref,
    keys_ref,
    weight_out,
    key_out,
    value_out,
    weight_all,
    high_ref,
    acc_ref,
    values_ref,
    out_sem,
    thin_local,
    thin_send,
    thin_recv,
    *sems,
):
    place = ring_place()
    y, core, _, _, sibling = place
    dp = lax.axis_index("dp")
    z, x = dp // N_X, dp % N_X
    up = {"dp": lax.rem(z + 1, RING) * N_X + x}
    down = {"dp": lax.rem(z + RING - 1, RING) * N_X + x}
    chips = [{"ctx": lax.rem(y + k, RING) * 2 + core} for k in range(1, RING)]
    greet(tuple(chips) + (sibling, up, down))
    depth = weight_ref.shape[0]
    low = depth // 2
    thin = low // RING
    high_rows = pl.ds(pl.multiple_of((z * 2 + core) * low, low), low)

    def thin_block(chip):
        start = (z * 2 + core) * low + lax.rem(chip + RING, RING) * thin
        return high_ref.at[pl.ds(pl.multiple_of(start, thin), thin), :]

    mine = weight_ref.at[pl.ds(pl.multiple_of(low + z * thin, thin), thin), :]

    def thin_copy(k, dst):
        return push(mine, dst, thin_send.at[k - 1], thin_recv.at[k - 1], chips[k - 1])

    thin_sent = [thin_copy(k, thin_block(y)) for k in range(1, RING)]
    for copy in thin_sent:
        copy.start()
    keep = pltpu.make_async_copy(mine, thin_block(y), thin_local)
    keep.start()

    weight = RingGather(
        0, weight_ref.at[pl.ds(0, low), :], weight_all, sems, place, stride=depth
    )
    high = RingGather(
        3, high_ref.at[high_rows, :], high_ref, sems, (z, core, up, down, sibling)
    )
    key = RingGather(1, keys_ref, key_out, sems, place)
    value = RingGather(2, values_ref, value_out, sems, place)

    def project(chip, which):
        start = (lax.rem(chip + RING, RING) * 2 + which) * depth
        rows = pl.ds(pl.multiple_of(start, low), low)
        acc_ref[...] += mm(hidden_ref[:, rows], weight_all[rows, :], NN)

    weight.start()
    acc_ref[...] = jnp.zeros_like(acc_ref)
    keep.wait()
    for k in range(1, RING):
        thin_copy(k, thin_block(y - k)).wait_recv()
    high.start(in_place=True)
    for step in range(STEPS):
        weight.step(step)
        if step == 1:
            key.start()
        high.step(step)
        if step == 0:
            weight.local.wait()
            project(y, core)
            weight.own_from_sibling()
            project(y, 1 - core)
        else:
            weight.from_sibling(step - 1)
            project(y - step, 1 - core)
            project(y + step, 1 - core)
        project(y - 1 - step, core)
        if step < STEPS - 1:
            project(y + 1 + step, core)
    key.step(0)
    weight.from_sibling(STEPS - 1)
    project(y + STEPS, 1 - core)
    high.own_from_sibling()
    for step in range(STEPS):
        high.from_sibling(step)
    for block in range(2 * RING):
        chip, which = block // 2, block % 2
        for layer in range(RING):
            src = (layer * 2 + which) * low + chip * thin
            dst = block * depth + low + layer * thin
            weight_all[dst : dst + thin, :] = high_ref[src : src + thin, :]
    total = acc_ref[...]
    for block in range(2 * RING):
        rows = slice(block * depth + low, (block + 1) * depth)
        total = total + mm(hidden_ref[:, rows], weight_all[rows, :], NN)
    values_ref[...] = total.astype(jnp.bfloat16)
    value.start()
    keep = pltpu.make_async_copy(weight_all, weight_out, out_sem)
    keep.start()
    for step in range(STEPS):
        if step + 1 < STEPS:
            key.step(step + 1)
        value.step(step)
    for each in (key, value):
        each.own_from_sibling()
        for step in range(STEPS):
            each.from_sibling(step)
    keep.wait()
    for each in (key, value):
        each.finish()
    for copy in weight.sent + high.sent + thin_sent:
        copy.wait_send()


def front(hidden, value_weight, keys, collective_id):
    tokens, kv_width = keys.shape
    ring = pltpu.SemaphoreType.DMA((4, 2, STEPS, 2))
    one = pltpu.SemaphoreType.DMA((4,))
    thin = pltpu.SemaphoreType.DMA((RING - 1,))
    anywhere = pl.BlockSpec(memory_space=pl.ANY)
    vmem = pl.BlockSpec(memory_space=pltpu.VMEM)
    depth = value_weight.shape[0] * 2 * RING
    gathered = jax.ShapeDtypeStruct((tokens * 2 * RING, kv_width), keys.dtype)
    return pl.pallas_call(
        front_kernel,
        out_shape=(
            jax.ShapeDtypeStruct((depth, kv_width), value_weight.dtype),
            gathered,
            gathered,
        ),
        in_specs=[vmem, vmem, vmem],
        out_specs=(anywhere,) * 3,
        scratch_shapes=[
            pltpu.VMEM((depth, kv_width), jnp.bfloat16),
            pltpu.VMEM((depth // 2, kv_width), jnp.bfloat16),
            pltpu.VMEM((tokens, kv_width), jnp.float32),
            pltpu.VMEM((tokens, kv_width), jnp.bfloat16),
            pltpu.SemaphoreType.DMA,
            pltpu.SemaphoreType.DMA,
            thin,
            thin,
            one,
            ring,
            ring,
            one,
            one,
            ring,
            ring,
        ],
        compiler_params=pltpu.CompilerParams(
            collective_id=collective_id,
            has_side_effects=True,
            vmem_limit_bytes=24 * 1024 * 1024,
        ),
        cost_estimate=pl.CostEstimate(
            flops=2 * tokens * depth * kv_width,
            bytes_accessed=4 * depth * kv_width,
            transcendentals=0,
        ),
        name="front",
    )(hidden, value_weight, keys)


NEAR = (4, 3, -3, 2, -2, 1, -1, 0)


class RingReduce:
    def __init__(self, term, send_ref, recv_ref, ring_send, ring_recv, place):
        self.term, self.send_ref, self.recv_ref = term, send_ref, recv_ref
        self.ring_send, self.ring_recv = ring_send, ring_recv
        self.targets = place[2:4]
        self.sent = []

    def copy(self, src, direction, step, half):
        return push(
            src,
            self.recv_ref.at[direction, step, half],
            self.ring_send.at[direction, step, half],
            self.ring_recv.at[direction, step, half],
            self.targets[direction],
        )

    def arrived(self, direction, step, half):
        self.copy(self.send_ref.at[direction, step, half], direction, step, half).wait_recv()
        return self.recv_ref[direction, step, half].astype(jnp.float32)

    def step(self, step):
        distance = STEPS - step
        for half in range(2):
            for direction in range(2):
                if not carried(direction, step, half, 0):
                    continue
                value = self.term(-distance if direction else distance, half)
                if step > 0 and carried(direction, step - 1, half, 0):
                    value = value + self.arrived(direction, step - 1, half)
                self.send_ref[direction, step, half] = value.astype(jnp.bfloat16)
                copy = self.copy(self.send_ref.at[direction, step, half], direction, step, half)
                copy.start()
                self.sent.append(copy)

    def result(self, half):
        value = self.term(0, half)
        for direction in range(2):
            value = value + self.arrived(direction, STEPS - 1, half)
        return value


class FromSibling:
    def __init__(self, land_ref, send_sem, recv_sem, sibling):
        self.land_ref, self.send_sem, self.recv_sem = land_ref, send_sem, recv_sem
        self.sibling = sibling
        self.sent = []
        self.waited = set()

    def copy(self, i, src):
        return push(
            src, self.land_ref.at[i], self.send_sem.at[i], self.recv_sem.at[i], self.sibling
        )

    def send(self, i, src):
        copy = self.copy(i, src)
        copy.start()
        self.sent.append(copy)

    def half_block(self, offset, half):
        i = NEAR.index(4 if offset == -4 else offset)
        if i not in self.waited:
            self.waited.add(i)
            self.copy(i, self.land_ref.at[i]).wait_recv()
        rows = self.land_ref.shape[1] // 2
        return self.land_ref[i, half * rows : (half + 1) * rows, :].astype(jnp.float32)


def back_kernel(
    terms_ref,
    hidden_ref,
    key_out,
    value_out,
    weight_out,
    t_land,
    t_send,
    t_recv,
    w_stage,
    w_land,
    w_send,
    w_recv,
    grads_ref,
    own_ref,
    z_land,
    part_ref,
    x_slots,
    total_ref,
    t_sib_send,
    t_sib_recv,
    t_ring_send,
    t_ring_recv,
    w_sib_send,
    w_sib_recv,
    w_ring_send,
    w_ring_recv,
    z_send,
    z_recv,
    x_send,
    x_recv,
    g_send,
    g_recv,
):
    place = ring_place()
    y, core = place[:2]
    sibling = place[4]
    dp = lax.axis_index("dp")
    z, x = dp // N_X, dp % N_X
    z_after = [{"dp": lax.rem(z + k, N_Z) * N_X + x} for k in range(1, N_Z)]
    x_after = [{"dp": z * N_X + lax.rem(x + k, N_X)} for k in range(1, N_X)]
    greet(tuple(place[2:]) + tuple(z_after) + tuple(x_after))

    tokens = hidden_ref.shape[0]
    width = key_out.shape[1]
    depth = own_ref.shape[0]

    def owner(offset, which):
        return lax.rem(y + offset + RING, RING) * 2 + which

    def term_sums(n, first_col):
        cols = slice(first_col, first_col + width)
        sib = FromSibling(t_land.at[n], t_sib_send.at[n], t_sib_recv.at[n], sibling)
        for i, offset in enumerate(NEAR):
            start = pl.multiple_of(owner(offset, 1 - core) * tokens, tokens)
            sib.send(i, terms_ref.at[pl.ds(start, tokens), cols])

        def term(offset, half):
            rows = tokens // 2
            start = pl.multiple_of(owner(offset, core) * tokens + half * rows, rows)
            mine = terms_ref[pl.ds(start, rows), cols].astype(jnp.float32)
            return mine + sib.half_block(offset, half)

        ring = RingReduce(
            term, t_send.at[n], t_recv.at[n], t_ring_send.at[n], t_ring_recv.at[n], place
        )
        return ring, sib

    value, value_sib = term_sums(0, width)
    key, key_sib = term_sums(1, 0)
    value.step(0)
    value.step(1)
    key.step(0)
    value.step(2)
    key.step(1)
    value.step(3)
    key.step(2)
    rows = tokens // 2
    for half in range(2):
        grads_ref[half * rows : (half + 1) * rows, :] = value.result(half).astype(jnp.bfloat16)

    def partial(offset, which, first_row, count):
        start = pl.multiple_of(owner(offset, which) * depth + first_row, count)
        return mm(hidden_ref[:, pl.ds(start, count)], grads_ref[...], TN)

    weight_sib = FromSibling(w_land, w_sib_send, w_sib_recv, sibling)

    def weight_term(offset, half):
        mine = partial(offset, core, half * (depth // 2), depth // 2)
        return mine + weight_sib.half_block(offset, half)

    weight = RingReduce(weight_term, w_send, w_recv, w_ring_send, w_ring_recv, place)

    def stage(*order):
        for i in order:
            w_stage[i] = partial(NEAR[i], 1 - core, 0, depth).astype(jnp.bfloat16)
            weight_sib.send(i, w_stage.at[i])

    stage(0, 1, 2)
    weight.step(0)
    key.step(3)
    stage(3, 4)
    weight.step(1)
    stage(5, 6, 7)
    weight.step(2)
    value_out[...] = grads_ref[...]
    for half in range(2):
        key_out[half * rows : (half + 1) * rows, :] = key.result(half).astype(jnp.bfloat16)
    weight.step(3)

    sent = value.sent + key.sent + weight.sent
    sent += value_sib.sent + key_sib.sent + weight_sib.sent
    half_depth = depth // 2
    part = half_depth // N_Z

    def z_rows(half, who):
        start = half * half_depth + lax.rem(who + N_Z, N_Z) * part
        return pl.ds(pl.multiple_of(start, part), part)

    def z_copy(half, k):
        return push(
            own_ref.at[z_rows(half, z + k), :],
            z_land.at[half, k - 1],
            z_send.at[half, k - 1],
            z_recv.at[half, k - 1],
            z_after[k - 1],
        )

    def x_copy(half, k, who):
        return push(
            part_ref.at[half],
            x_slots.at[half, lax.rem(who + N_X, N_X)],
            x_send.at[half, k - 1],
            x_recv.at[half, k - 1],
            x_after[k - 1],
        )

    def g_copy(half, k, who):
        there = total_ref.at[z_rows(half, who), :]
        return push(
            there, there, g_send.at[half, k - 1], g_recv.at[half, k - 1], z_after[k - 1]
        )

    for half in range(2):
        own_ref[half * half_depth : (half + 1) * half_depth, :] = weight.result(half).astype(
            jnp.bfloat16
        )
        for k in range(1, N_Z):
            copy = z_copy(half, k)
            copy.start()
            sent.append(copy)
    for half in range(2):
        total = own_ref[z_rows(half, z), :].astype(jnp.float32)
        for k in range(1, N_Z):
            z_copy(half, k).wait_recv()
            total = total + z_land[half, k - 1].astype(jnp.float32)
        part_ref[half] = total.astype(jnp.bfloat16)
        x_slots[half, x] = part_ref[half]
        for k in range(1, N_X):
            copy = x_copy(half, k, x)
            copy.start()
            sent.append(copy)
    for half in range(2):
        for k in range(1, N_X):
            x_copy(half, k, x - k).wait_recv()
        total = x_slots[half, 0].astype(jnp.float32)
        for k in range(1, N_X):
            total = total + x_slots[half, k].astype(jnp.float32)
        total_ref[z_rows(half, z), :] = (total * (1.0 / (N_Z * N_X))).astype(jnp.bfloat16)
        for k in range(1, N_Z):
            copy = g_copy(half, k, z)
            copy.start()
            sent.append(copy)
    for half in range(2):
        for k in range(1, N_Z):
            g_copy(half, k, z - k).wait_recv()
    weight_out[...] = total_ref[...]
    for copy in sent:
        copy.wait_send()


def back(terms, hidden, collective_id):
    tokens, features = hidden.shape
    width = terms.shape[1] // 2
    depth = features // (2 * RING)
    part = depth // 2 // N_Z
    vmem = pl.BlockSpec(memory_space=pltpu.VMEM)

    def buffer(*shape):
        return pltpu.VMEM(shape, jnp.bfloat16)

    def dma(*shape):
        return pltpu.SemaphoreType.DMA(shape)

    t_slots = buffer(2, 2, STEPS, 2, tokens // 2, width)
    w_slots = buffer(2, STEPS, 2, depth // 2, width)
    return pl.pallas_call(
        back_kernel,
        out_shape=(
            jax.ShapeDtypeStruct((tokens, width), jnp.bfloat16),
            jax.ShapeDtypeStruct((tokens, width), jnp.bfloat16),
            jax.ShapeDtypeStruct((depth, width), jnp.bfloat16),
        ),
        in_specs=[vmem, vmem],
        out_specs=(vmem,) * 3,
        scratch_shapes=[
            buffer(2, RING, tokens, width),
            t_slots,
            t_slots,
            buffer(RING, depth, width),
            buffer(RING, depth, width),
            w_slots,
            w_slots,
            buffer(tokens, width),
            buffer(depth, width),
            buffer(2, N_Z - 1, part, width),
            buffer(2, part, width),
            buffer(2, N_X, part, width),
            buffer(depth, width),
            dma(2, RING),
            dma(2, RING),
            dma(2, 2, STEPS, 2),
            dma(2, 2, STEPS, 2),
            dma(RING),
            dma(RING),
            dma(2, STEPS, 2),
            dma(2, STEPS, 2),
            dma(2, N_Z - 1),
            dma(2, N_Z - 1),
            dma(2, N_X - 1),
            dma(2, N_X - 1),
            dma(2, N_Z - 1),
            dma(2, N_Z - 1),
        ],
        compiler_params=pltpu.CompilerParams(
            collective_id=collective_id,
            has_side_effects=True,
            vmem_limit_bytes=36 * 1024 * 1024,
        ),
        cost_estimate=pl.CostEstimate(
            flops=2 * hidden.size * width, bytes_accessed=4 * terms.size, transcendentals=0
        ),
        name="back",
    )(terms, hidden)


def per_device(hidden, queries, keys, cotangent, value_weight, doc_ids, span_order):
    rank_index = lax.axis_index("ctx")
    token_rows = hidden[0]
    weight_all, key_all, value_all = front(token_rows, value_weight, keys[0], 0)
    attention_out, query_grads, kv_terms = attention(
        queries[0], cotangent[0], key_all, value_all, doc_ids[0], span_order[0], rank_index
    )
    key_own, value_own, weight_grads = back(kv_terms, token_rows, 1)
    input_grads = lax.dot_general(
        value_own, weight_all, NT, preferred_element_type=jnp.float32
    ).astype(jnp.bfloat16)
    return (
        attention_out[None],
        query_grads[None],
        key_own[None],
        input_grads[None],
        weight_grads,
    )


def solution(mesh):
    return jax.shard_map(
        per_device,
        mesh=mesh,
        in_specs=(
            P("dp", "ctx", None),
            P("dp", "ctx", None),
            P("dp", "ctx", None),
            P("dp", "ctx", None),
            P("ctx", None),
            P("dp", None),
            P("dp", None),
        ),
        out_specs=(
            P("dp", "ctx", None),
            P("dp", "ctx", None),
            P("dp", "ctx", None),
            P("dp", "ctx", None),
            P("ctx", None),
        ),
        check_vma=False,
    )
```
